128 devices in a mesh: row: 8 (over z, core), col: 16 (over x, y).
Axes of the slice: x: 4, y: 4, z: 4, core: 2. Of those that a mesh axis runs over, the one named last changes fastest.
Arguments:
- front_matrix: float32 [16384, 16384], P('row', 'col'), may hold values from -168 to 3072, as said below
- child_blocks: float32 [1024, 256, 256], P(('row', 'col')), may hold values from -3 to 3
- child_target: int32 [1024, 2], P(('row', 'col')), may hold values from 8 to 63, as said below
- child_place: int32 [1024, 2, 256], P(('row', 'col')), may hold values from 0 to 255, as said below
- child_live: int32 [1024, 2], P(('row', 'col')), may hold values from 128 to 256
Outputs:
- factored: float32 [16384, 16384], P('row', 'col')
The draws below stay inside these ranges and needn't reach their ends.
Inputs may be any that keep to these rules, and one draw needn't show every extreme that they name: The block of front_matrix on the first 1024 front rows and columns is symmetric positive definite, with smallest eigenvalue at least 0.3 * 2 * 2 * 256. child_target[k,0] leaves the same remainder modulo 8 as the mesh row of the device holding block k, and is at least 8; child_target[k,1] is at least 16; the blocks held by one device name at most 2 distinct blocks whose column leaves one remainder modulo 16, and in every mesh row some remainder receives 2 blocks from every device of that row. Each row child_place[k,i,:] is a permutation of 0 .. 255.
All inputs are finite; a program needn't handle non-finite values.
Results may differ from the reference program's by a relative error of at most 0.0003.
Values sent between devices are 32-bit elements; how exact they have to be, the bound alone decides.
No kernel may reach another device: no remote copies, remote signals or barrier semaphores. Data moves between devices by JAX's collectives and lax.ppermute only.
A program may use at most 128 MiB of HBM per device.

```python
import jax
import jax.numpy as jnp
from jax import lax

BLK = 256
PBLK = 2
NPAN = 2
MB_COL = 4
CAP = 2
KID_DEV = 8
MB_ROW = 8
NF = 16384
KIDS = 1024


def draw_front_matrix(key, part):
    key = jax.random.fold_in(key, 1)
    rows_dev = MB_ROW * BLK
    cols_dev = MB_COL * BLK
    mesh_rows = NF // rows_dev
    mesh_cols = NF // cols_dev
    index = jnp.arange(NF, dtype=jnp.int32)
    front_row = (index % rows_dev // BLK * mesh_rows + index // rows_dev) * BLK + index % BLK
    front_col = (index % cols_dev // BLK * mesh_cols + index // cols_dev) * BLK + index % BLK
    first_key = jax.random.fold_in(key, 0)
    second_key = jax.random.fold_in(key, 1)
    fourth_key = jax.random.fold_in(key, 3)
    base = jax.random.uniform(first_key, (NF, NF), jnp.float32, -1.0, 1.0)
    leading = NPAN * PBLK * BLK
    generator = jax.random.uniform(fourth_key, (leading, leading), jnp.float32, -1.0, 1.0)
    diagonal_part = jax.random.uniform(second_key, (leading,), jnp.float32, 0.2, 0.5)
    gram_part = jnp.dot(generator, generator.T, precision=lax.Precision.HIGHEST, preferred_element_type=jnp.float32) / leading
    lead_block = 1.5 * leading * (gram_part + jnp.diag(diagonal_part))
    clip_row = jnp.minimum(front_row, leading - 1)
    clip_col = jnp.minimum(front_col, leading - 1)
    lead_full = lead_block[clip_row][:, clip_col]
    row_scale = jnp.ones((NF,), jnp.float32)
    row_grid = front_row[:, None]
    col_grid = front_col[None, :]
    result = jnp.where((row_grid >= leading) & (col_grid < leading), base * (20.0 * row_scale[:, None]), base)
    result = jnp.where((row_grid >= leading) & (col_grid >= leading), result, result)
    result = jnp.where((row_grid < leading) & (col_grid < leading), lead_full, result)
    return result.astype(jnp.float32)


def draw_child_target(key, part):
    key = jax.random.fold_in(key, 2)
    devices = KIDS // KID_DEV
    mesh_rows = NF // (MB_ROW * BLK)
    mesh_cols = devices // mesh_rows
    hot_key, perm_key, row_key, col_key, order_key = jax.random.split(key, 5)
    hot = jax.random.randint(hot_key, (mesh_rows,), 0, mesh_cols)
    device_row = jnp.arange(devices, dtype=jnp.int32) // mesh_cols
    device_hot = hot[device_row]
    slot_total = mesh_cols * CAP
    perms = jax.vmap(lambda k: jax.random.permutation(k, slot_total))(jax.random.split(perm_key, devices))
    slot_col = jnp.arange(slot_total, dtype=jnp.int32) // CAP
    scores = perms + jnp.where(slot_col[None, :] == device_hot[:, None], slot_total, 0)
    ordered = jnp.argsort(scores, axis=1, stable=True)[:, :KID_DEV - CAP]
    other_cols = (ordered // CAP).astype(jnp.int32)
    hot_cols = jnp.broadcast_to(device_hot[:, None], (devices, CAP)).astype(jnp.int32)
    columns = jnp.concatenate([hot_cols, other_cols], axis=1)
    shuffle = jax.vmap(lambda k: jax.random.permutation(k, KID_DEV))(jax.random.split(order_key, devices))
    columns = jnp.take_along_axis(columns, shuffle, axis=1)
    row_step = jax.random.randint(row_key, (devices, KID_DEV), 1, MB_ROW)
    col_step = jax.random.randint(col_key, (devices, KID_DEV), 1, MB_COL)
    target_row = device_row[:, None] + mesh_rows * row_step
    target_col = columns + mesh_cols * col_step
    return jnp.stack([target_row, target_col], axis=2).reshape(KIDS, 2).astype(jnp.int32)


def draw_child_place(key, part):
    key = jax.random.fold_in(key, 3)
    perms = jax.vmap(lambda k: jax.random.permutation(k, BLK))(jax.random.split(key, KIDS * 2))
    return perms.reshape(KIDS, 2, BLK).astype(jnp.int32)


def touch_ends(values, own_key, low, top_value):
    longest = values.shape.index(max(values.shape))
    spots = []
    for shift in (0, 1):
        where = [jax.random.randint(jax.random.fold_in(own_key, axis), (), 0, length) for axis, length in enumerate(values.shape)]
        where[longest] = (where[longest] + shift) % values.shape[longest]
        spots.append(tuple(where))
    return values.at[spots[0]].set(low).at[spots[1]].set(top_value)


def levels(stream_key, shape, shards, smallest, largest):
    gain = 1.0
    for position, blocks in shards:
        steps = jax.random.uniform(jax.random.fold_in(jax.random.fold_in(stream_key, 6), position), (blocks,), jnp.float32, smallest / len(shards), largest / len(shards))
        gain = gain * jnp.repeat(jnp.exp(steps), shape[position] // blocks).reshape((-1,) + (1,) * (len(shape) - 1 - position))
    return gain


def gaussian(own_key, extent, deviation, limit, pieces=(), kind=jnp.bfloat16):
    values = jax.random.normal(own_key, extent, jnp.float32) * deviation
    if len(pieces) > 0:
        values = levels(own_key, extent, pieces, -0.22, 0.18) * values
    return jnp.clip(values, min=-limit, max=limit).astype(kind)


def setup_inputs(seed: int = 0) -> dict:
    keys = jax.random.split(jax.random.key(seed), 6)
    return {
        "front_matrix": draw_front_matrix(jax.random.fold_in(keys[5], 71), 0),
        "child_blocks": gaussian(keys[1], (KIDS, BLK, BLK), 0.5, 3.0, ((0, 128),), jnp.float32),
        "child_target": draw_child_target(jax.random.fold_in(keys[5], 71), 0),
        "child_place": draw_child_place(jax.random.fold_in(keys[5], 71), 0),
        "child_live": touch_ends(jax.random.randint(keys[4], (KIDS, 2), BLK // 2, BLK + 1), jax.random.fold_in(keys[4], 1), BLK // 2, BLK).astype(jnp.int32),
    }


def front_order(total, slots):
    mesh_count = total // (slots * BLK)
    index = jnp.arange(total, dtype=jnp.int32)
    fblock = index // BLK
    return (fblock % mesh_count * (slots * BLK) + fblock // mesh_count * BLK + index % BLK).astype(jnp.int32)

def storage_order(total, slots):
    mesh_count = total // (slots * BLK)
    index = jnp.arange(total, dtype=jnp.int32)
    within = index % (slots * BLK)
    return ((within // BLK * mesh_count + index // (slots * BLK)) * BLK + index % BLK).astype(jnp.int32)

def map_child(values, place, live):
    counter = jnp.arange(BLK, dtype=jnp.int32)
    active = (counter < live[0])[:, None] & (counter < live[1])[None, :]
    masked = jnp.where(active, values, jnp.zeros_like(values))
    return jnp.zeros((BLK, BLK), jnp.float32).at[place[0][:, None], place[1][None, :]].add(masked)

def reference(front_matrix, child_blocks, child_target, child_place, child_live):
    matrix = front_matrix[front_order(NF, MB_ROW)][:, front_order(NF, MB_COL)]
    mapped = jax.vmap(map_child)(child_blocks, child_place, child_live)

    def add_child(number, acc):
        start_row = (child_target[number, 0] * BLK).astype(jnp.int32)
        start_col = (child_target[number, 1] * BLK).astype(jnp.int32)
        current = lax.dynamic_slice(acc, (start_row, start_col), (BLK, BLK))
        return lax.dynamic_update_slice(acc, current + mapped[number], (start_row, start_col))
    matrix = lax.fori_loop(0, KIDS, add_child, matrix)
    width = PBLK * BLK
    for panel in range(NPAN):
        lower = panel * width
        upper = lower + width
        pivot = matrix[lower:upper, lower:upper]
        pivot = jnp.tril(pivot) + jnp.tril(pivot, -1).T
        factor = jnp.linalg.cholesky(pivot)
        below = jax.scipy.linalg.solve_triangular(factor, matrix[upper:, lower:upper].T, lower=True).T
        matrix = matrix.at[:lower, lower:upper].set(jnp.float32(0.0))
        matrix = matrix.at[lower:upper, lower:upper].set(factor)
        matrix = matrix.at[upper:, lower:upper].set(below)
        update = jnp.dot(below.astype(jnp.float32), below.T.astype(jnp.float32), precision=lax.Precision.HIGHEST, preferred_element_type=jnp.float32)
        matrix = matrix.at[upper:, upper:].set(matrix[upper:, upper:] - update)
    return matrix[storage_order(NF, MB_ROW)][:, storage_order(NF, MB_COL)]
```

```python
import jax
import jax.numpy as jnp
from jax import lax
from jax.experimental import pallas as pl
from jax.experimental.pallas import tpu as pltpu
from jax.sharding import PartitionSpec as P

F32 = jnp.float32
BF16 = jnp.bfloat16
I32 = jnp.int32
BLK = 256
LEADS = 4
CAP = 2
SIDE = 4
NB = 128
HIGHEST = lax.Precision.HIGHEST


def dot_nt(left, right, precision=None):
    return lax.dot_general(
        left, right, (((1,), (1,)), ((), ())), precision=precision, preferred_element_type=F32
    )


def dot_nn(left, right, precision=None):
    return lax.dot_general(
        left, right, (((1,), (0,)), ((), ())), precision=precision, preferred_element_type=F32
    )


def split2(value):
    high = value.astype(BF16)
    return high, (value - high.astype(F32)).astype(BF16)


def shift_xy(value, dx, dy):
    pairs = []
    for x in range(SIDE):
        for y in range(SIDE):
            pairs.append((x * SIDE + y, (x + dx) % SIDE * SIDE + (y + dy) % SIDE))
    return lax.ppermute(value, "col", pairs)


def shift_z(value, dz):
    return lax.ppermute(value, "row", [(r, (r + 2 * dz) % 8) for r in range(8)])


def swap_cores(value):
    return lax.ppermute(value, "row", [(r, r ^ 1) for r in range(8)])


def ring_gather(value, shift):
    half = value.shape[0] // 2
    before = shift(value, 1)
    after = shift(value, -1)
    far = jnp.concatenate([shift(before[:half], 1), shift(after[half:], -1)], axis=0)
    return jnp.stack([value, before, after, far])


def along_x(value, step):
    return shift_xy(value, step, 0)


def along_y(value, step):
    return shift_xy(value, 0, step)


def ring_place(delta):
    delta = delta % SIDE
    return jnp.where(delta == 0, 0, jnp.where(delta == 1, 2, jnp.where(delta == 2, 3, 1))).astype(I32)


def flat(value, keep):
    return value.reshape((-1,) + value.shape[value.ndim - keep :])


def spread_x(parts, x):
    out = jnp.where(x == 0, parts[0], jnp.zeros_like(parts[0]))
    for q in range(1, SIDE):
        out = out + lax.ppermute(parts[q], "col", [(y, q * SIDE + y) for y in range(SIDE)])
    return out


def gather_lead(block, x, z):
    rows = block.shape[0] // SIDE
    piece = spread_x([block[q * rows : (q + 1) * rows] for q in range(SIDE)], x)

    def from_low(value, dz):
        pairs = [((2 * s + k), (2 * (s + dz) + k) % 8) for s in range(2) for k in range(2)]
        return lax.ppermute(value, "row", pairs)

    up, down, far = from_low(piece, 1), from_low(piece, -1), from_low(piece, 2)
    plane0 = jnp.where(z == 0, piece, jnp.where(z == 1, up, jnp.where(z == 2, far, down)))
    plane1 = jnp.where(z == 1, piece, jnp.where(z == 2, up, jnp.where(z == 3, far, down)))
    mine = jnp.stack([plane0, plane1])
    other = swap_cores(mine)
    core = lax.axis_index("row") % 2
    even = jnp.where(core == 0, mine, other)
    odd = jnp.where(core == 0, other, mine)
    four = jnp.stack([even[0], odd[0], even[1], odd[1]])
    half = rows // 2
    share = lax.dynamic_slice_in_dim(four, core * half, half, axis=1)
    first = ring_gather(flat(ring_gather(share[:2], along_x), 2), along_y)
    second = ring_gather(flat(ring_gather(share[2:], along_y), 2), along_x)
    both = jnp.concatenate([flat(first, 2), flat(second, 2)], axis=0)
    return both, swap_cores(both)


def gather_rows(slab, x):
    rows = slab.shape[0] // SIDE
    piece = spread_x([slab[q * rows : (q + 1) * rows] for q in range(SIDE)], x)
    first, second = piece[: rows // 2], piece[rows // 2 :]
    first = ring_gather(flat(ring_gather(first, along_x), 2).reshape(SIDE, BLK, BLK), along_y)
    second = ring_gather(flat(ring_gather(second, along_y), 2).reshape(SIDE, BLK, BLK), along_x)
    return flat(first, 2), flat(second, 2)


def gather_cols(slab):
    blocks = slab.reshape(8, BLK, BLK)
    out = None
    for h in range(2):
        for q in range(2):
            pairs = []
            for r in range(8):
                for j in range(LEADS):
                    pairs.append((r * 16 + j, (2 * j + q) * 16 + r + 8 * h))
            part = jnp.stack([blocks[4 * q + h], blocks[4 * q + 2 + h]])
            part = lax.ppermute(part, ("row", "col"), pairs)
            out = part if out is None else out + part
    own = flat(ring_gather(out, shift_z), 2)
    return jnp.concatenate([own, swap_cores(own)], axis=0)


def factor_block(a, u_ref, e_ref):
    n = a.shape[0]
    ri = lax.broadcasted_iota(I32, (n, n), 0)
    ci = lax.broadcasted_iota(I32, (n, n), 1)
    e = jnp.where(ri == ci, F32(1), F32(0))
    base = 0
    for p in range(0, n, 4):
        off = p - base
        m = a.shape[0]
        cols = [jnp.broadcast_to(a[:, p + v : p + v + 1], (m, n)) for v in range(4)]
        s = [[cols[v][off + i : off + i + 1, :] for v in range(4)] for i in range(4)]
        arow = [a[off + i : off + i + 1, :] for i in range(4)]
        erow = [e[off + i : off + i + 1, :] for i in range(4)]
        inverse = []
        for q in range(4):
            r = F32(1) / s[q][q]
            inverse.append(r)
            low = [None] * 4
            for i in range(q + 1, 4):
                low[i] = s[i][q] * r
            for i in range(q + 1, 4):
                for v in range(q + 1, i + 1):
                    s[i][v] = s[i][v] - low[i] * s[v][q]
                arow[i] = arow[i] - low[i] * arow[q]
                erow[i] = erow[i] - low[i] * erow[q]
        for q in range(4):
            scale = lax.rsqrt(s[q][q])
            u_ref[p + q : p + q + 1, :] = arow[q] * scale
            e_ref[p + q : p + q + 1, :] = erow[q] * scale
        following = p + 4
        if following >= n:
            break
        live = None
        if following % 8 == 0:
            cut = following - base
            a, e, cols = a[cut:], e[cut:], [c[cut:] for c in cols]
            base = following
        else:
            live = lax.broadcasted_iota(I32, a.shape, 0) >= following - base
        times = []
        for q in range(4):
            c = cols[q]
            for v in range(q):
                c = c - times[v] * s[q][v]
            times.append(c * inverse[q])
        da = times[0] * arow[0]
        de = times[0] * erow[0]
        for q in range(1, 4):
            da = da + times[q] * arow[q]
            de = de + times[q] * erow[q]
        if live is not None:
            da = jnp.where(live, da, F32(0))
            de = jnp.where(live, de, F32(0))
        a = a - da
        e = e - de


def factor_kernel(table, own_ref, other_ref, l_ref, inv_ref, m_ref, u_ref, e_ref):
    n = m_ref.shape[0]
    steps = n // NB
    half = 32

    def assemble(sources):
        def place(number, carry):
            xx, yy = number // SIDE, number % SIDE
            for i in range(LEADS):
                at = table[number] if i < 2 else table[16 + number]
                for h in range(2):
                    row = pl.multiple_of(i * BLK + xx * 2 * half + h * half, half)
                    col = pl.multiple_of(yy * BLK, BLK)
                    m_ref[pl.ds(row, half), pl.ds(col, BLK)] = sources[h][at * 2 + i % 2]
            return carry

        lax.fori_loop(0, SIDE * SIDE, place, 0)

    @pl.when(table[32] == 0)
    def _():
        assemble((own_ref, other_ref))

    @pl.when(table[32] != 0)
    def _():
        assemble((other_ref, own_ref))

    l_ref[...] = jnp.zeros_like(l_ref)
    ri = lax.broadcasted_iota(I32, (NB, NB), 0)
    ci = lax.broadcasted_iota(I32, (NB, NB), 1)

    def step(k, carry):
        at = pl.multiple_of(k * NB, NB)
        d = m_ref[pl.ds(at, NB), pl.ds(at, NB)]
        factor_block(jnp.where(ri >= ci, d, d.T), u_ref, e_ref)
        l_ref[pl.ds(at, NB), pl.ds(at, NB)] = jnp.where(ri <= ci, u_ref[...], F32(0)).T
        ik = jnp.where(ri >= ci, e_ref[...], F32(0))
        for kk in range(steps):

            @pl.when(k == kk)
            def _():
                lo, hi = kk * NB, (kk + 1) * NB
                if kk < steps - 1:
                    panel = dot_nt(m_ref[hi:, lo:hi], ik, HIGHEST)
                    l_ref[hi:, lo:hi] = panel
                    m_ref[hi:, hi:] = m_ref[hi:, hi:] - dot_nt(panel, panel, HIGHEST)
                b, h = kk // 2, kk % 2 * NB
                inv_ref[b, h : h + NB, h : h + NB] = ik
                if kk % 2 == 0:
                    inv_ref[b, :NB, NB:] = jnp.zeros((NB, NB), F32)
                else:
                    left = dot_nn(l_ref[lo:hi, lo - NB : lo], inv_ref[b, :NB, :NB], HIGHEST)
                    inv_ref[b, NB:, :NB] = -dot_nn(ik, left, HIGHEST)

        return carry

    lax.fori_loop(0, steps, step, 0)


def factor_lead(table, own, other):
    n = LEADS * BLK
    vmem = pl.BlockSpec(memory_space=pltpu.VMEM)
    return pl.pallas_call(
        factor_kernel,
        out_shape=(
            jax.ShapeDtypeStruct((n, n), F32),
            jax.ShapeDtypeStruct((LEADS, BLK, BLK), F32),
        ),
        in_specs=[pl.BlockSpec(memory_space=pltpu.SMEM), vmem, vmem],
        out_specs=[vmem, vmem],
        scratch_shapes=[
            pltpu.VMEM((n, n), F32),
            pltpu.VMEM((NB, NB), F32),
            pltpu.VMEM((NB, NB), F32),
        ],
        compiler_params=pltpu.CompilerParams(vmem_limit_bytes=40 << 20),
        cost_estimate=pl.CostEstimate(flops=60_000_000_000, bytes_accessed=10 << 20, transcendentals=0),
        name="factor_lead",
    )(table, own, other)


def update_kernel(table, *refs):
    uc, ta, tb = refs[0:4], refs[4:8], refs[8:12]
    front_ref, l_ref, inv_ref, out_ref = refs[12:16]
    lh, ll, dh, dl, ch, cl, uh, ul, pan = refs[16:]
    g = pl.program_id(0)
    r, c = table[48], table[49]

    @pl.when(g == 0)
    def _():
        for i in range(LEADS):
            rows = slice(i * BLK, (i + 1) * BLK)
            lh[rows, :], ll[rows, :] = split2(l_ref[rows, :])
            dh[i], dl[i] = split2(inv_ref[i])

    def solve(raw):
        for j in range(LEADS):
            cols = slice(j * BLK, (j + 1) * BLK)
            acc = raw[j][0]
            if j > 0:
                done = slice(0, j * BLK)
                left_h, left_l = uh[:, done], ul[:, done]
                low_h, low_l = lh[cols, done], ll[cols, done]
                acc = acc - (
                    dot_nt(left_h, low_h) + (dot_nt(left_h, low_l) + dot_nt(left_l, low_h))
                )
            acc_h, acc_l = split2(acc)
            got = dot_nt(acc_h, dh[j]) + (dot_nt(acc_h, dl[j]) + dot_nt(acc_l, dh[j]))
            uh[:, cols], ul[:, cols] = split2(got)

            @pl.when(c == j)
            def _():
                pan[...] = got

    @pl.when(g < 4)
    def _():
        solve(uc)
        at = pl.ds(pl.multiple_of(g * BLK, BLK), BLK)
        ch[at, :] = uh[...]
        cl[at, :] = ul[...]

    @pl.when((g >= 4) & (g % 2 == 0))
    def _():
        solve(ta)

    @pl.when((g >= 4) & (g % 2 == 1))
    def _():
        solve(tb)

    @pl.when((g == 4) & (r < LEADS))
    def _():
        at = pl.ds(pl.multiple_of(r * BLK, BLK), BLK)
        keep = jnp.where(r >= 2, 1.0, 0.0).astype(BF16)
        uh[:, : 2 * BLK] = lh[at, : 2 * BLK] * keep
        ul[:, : 2 * BLK] = ll[at, : 2 * BLK] * keep
        uh[:, 2 * BLK :] = jnp.zeros((BLK, 2 * BLK), BF16)
        ul[:, 2 * BLK :] = jnp.zeros((BLK, 2 * BLK), BF16)
        for j in range(LEADS):

            @pl.when(c == j)
            def _():
                pan[...] = l_ref[at, j * BLK : (j + 1) * BLK]

    @pl.when(g >= 4)
    def _():
        left_h, left_l = uh[...], ul[...]
        for t in range(4):
            rows = slice(t * BLK, (t + 1) * BLK)
            right_h, right_l = ch[rows, :], cl[rows, :]
            out_ref[:, rows] = front_ref[:, rows] - (
                dot_nt(left_h, right_h) + (dot_nt(left_h, right_l) + dot_nt(left_l, right_h))
            )

        @pl.when(c < LEADS)
        def _():
            out_ref[:, :BLK] = pan[...]


def update_front(table, uc, ta, tb, front, factor, inverse):
    n = LEADS * BLK
    rows, cols = front.shape

    def slot(g):
        return jnp.maximum(g - 4, 0)

    def uc_spec(j):
        return pl.BlockSpec((1, BLK, BLK), lambda g, t: (t[32 + jnp.minimum(g, 3) * 4 + j], 0, 0))

    def raw_spec(start, j):
        return pl.BlockSpec((1, BLK, BLK), lambda g, t: (t[start + slot(g) // 2 * 4 + j], 0, 0))

    in_specs = [uc_spec(j) for j in range(4)]
    in_specs += [raw_spec(0, j) for j in range(4)]
    in_specs += [raw_spec(16, j) for j in range(4)]
    in_specs += [
        pl.BlockSpec((BLK, cols), lambda g, t: (slot(g), 0)),
        pl.BlockSpec((n, n), lambda g, t: (0, 0)),
        pl.BlockSpec((LEADS, BLK, BLK), lambda g, t: (0, 0, 0)),
    ]
    return pl.pallas_call(
        update_kernel,
        out_shape=jax.ShapeDtypeStruct((rows, cols), F32),
        grid_spec=pltpu.PrefetchScalarGridSpec(
            num_scalar_prefetch=1,
            grid=(4 + rows // BLK,),
            in_specs=in_specs,
            out_specs=pl.BlockSpec((BLK, cols), lambda g, t: (slot(g), 0)),
            scratch_shapes=[
                pltpu.VMEM((n, n), BF16),
                pltpu.VMEM((n, n), BF16),
                pltpu.VMEM((LEADS, BLK, BLK), BF16),
                pltpu.VMEM((LEADS, BLK, BLK), BF16),
                pltpu.VMEM((n, n), BF16),
                pltpu.VMEM((n, n), BF16),
                pltpu.VMEM((BLK, n), BF16),
                pltpu.VMEM((BLK, n), BF16),
                pltpu.VMEM((BLK, BLK), F32),
            ],
        ),
        compiler_params=pltpu.CompilerParams(vmem_limit_bytes=56 << 20),
        cost_estimate=pl.CostEstimate(flops=26_000_000_000, bytes_accessed=36 << 20, transcendentals=0),
        name="update_front",
    )(table, *([uc] * 4), *([ta] * 4), *([tb] * 4), front, factor, inverse)


def slots_of(target, mesh_cols):
    kids = target.shape[-2]
    same = jnp.all(target[..., :, None, :] == target[..., None, :, :], axis=-1)
    number = jnp.arange(kids, dtype=I32)
    first = jnp.min(jnp.where(same, number, kids), axis=-1)
    leads = first == number
    goal = target[..., 1] % mesh_cols
    alike = (goal[..., :, None] == goal[..., None, :]) & leads[..., None, :]
    rank = jnp.sum((alike & (number < first[..., :, None])).astype(I32), axis=-1)
    return goal * CAP + rank, leads


def sort_order(keys):
    count = keys.shape[0]
    number = jnp.arange(count, dtype=I32)
    before = (keys[None, :] < keys[:, None]) | (
        (keys[None, :] == keys[:, None]) & (number[None, :] < number[:, None])
    )
    place = jnp.sum(before.astype(I32), axis=1)
    hot = (place[None, :] == number[:, None]).astype(I32)
    return lambda values: jnp.sum(hot * values[None, :], axis=1)


def map_kernel(table, block_ref, place_ref, out_ref):
    k = pl.program_id(0)
    live_row, live_col = table[16 + k], table[24 + k]
    target = lax.broadcasted_iota(I32, (BLK, BLK), 0)
    source = lax.broadcasted_iota(I32, (BLK, BLK), 1)

    def picks(index, live):
        hit = (place_ref[0, index : index + 1, :] == target) & (source < live)
        return jnp.where(hit, F32(1), F32(0)).astype(BF16)

    def parts(value):
        high = value.astype(BF16)
        rest = value - high.astype(F32)
        middle = rest.astype(BF16)
        return high, middle, (rest - middle.astype(F32)).astype(BF16)

    row_pick, col_pick = picks(0, live_row), picks(1, live_col)
    high, middle, low = parts(block_ref[0])
    moved = dot_nn(row_pick, high) + (dot_nn(row_pick, middle) + dot_nn(row_pick, low))
    high, middle, low = parts(moved)
    mapped = dot_nt(high, col_pick) + (dot_nt(middle, col_pick) + dot_nt(low, col_pick))
    opens = (k == 0) | (table[8 + k] != table[8 + jnp.maximum(k - 1, 0)])

    @pl.when(opens)
    def _():
        out_ref[0] = mapped

    @pl.when(jnp.logical_not(opens))
    def _():
        out_ref[0] = out_ref[0] + mapped


def map_children(child_blocks, child_target, child_place, child_live, mesh_cols):
    kids = child_blocks.shape[0]
    slot, _ = slots_of(child_target, mesh_cols)
    ordered = sort_order(slot)
    table = jnp.concatenate(
        [
            ordered(jnp.arange(kids, dtype=I32)),
            ordered(slot),
            ordered(child_live[:, 0]),
            ordered(child_live[:, 1]),
        ]
    )
    return pl.pallas_call(
        map_kernel,
        out_shape=jax.ShapeDtypeStruct((mesh_cols * CAP, BLK, BLK), F32),
        grid_spec=pltpu.PrefetchScalarGridSpec(
            num_scalar_prefetch=1,
            grid=(kids,),
            in_specs=[
                pl.BlockSpec((1, BLK, BLK), lambda k, t: (t[k], 0, 0)),
                pl.BlockSpec((1, 2, BLK), lambda k, t: (t[k], 0, 0)),
            ],
            out_specs=pl.BlockSpec((1, BLK, BLK), lambda k, t: (t[8 + k], 0, 0)),
        ),
        cost_estimate=pl.CostEstimate(flops=2_000_000_000, bytes_accessed=4 << 20, transcendentals=0),
        name="map_children",
    )(table, child_blocks, child_place)


def add_kernel(table, base_ref, slot_ref, out_ref):
    n = pl.program_id(0)
    total = 32
    opens = (n == 0) | (table[n] != table[jnp.maximum(n - 1, 0)])
    valid = n < table[2 * total]

    @pl.when(opens & valid)
    def _():
        out_ref[...] = base_ref[...] + slot_ref[0]

    @pl.when(opens & jnp.logical_not(valid))
    def _():
        out_ref[...] = base_ref[...]

    @pl.when(jnp.logical_not(opens) & valid)
    def _():
        out_ref[...] = out_ref[...] + slot_ref[0]


def add_table(targets, mesh_rows, mesh_cols, column):
    slot, leads = slots_of(targets, mesh_cols)
    mine = leads & (targets[..., 1] % mesh_cols == column)
    tile = targets[..., 0] // mesh_rows * 4 + targets[..., 1] // mesh_cols
    rank = slot % CAP
    keys = []
    for q in range(CAP):
        here = mine & (rank == q)
        keys.append(jnp.sum(jnp.where(here, tile + 1, 0), axis=1))
    key = jnp.stack(keys, axis=1).reshape(-1)
    total = key.shape[0]
    valid = key > 0
    count = jnp.sum(valid.astype(I32))
    ordered = sort_order(jnp.where(valid, key, 1 << 20))
    tiles = ordered(jnp.maximum(key - 1, 0))
    slots = ordered(jnp.arange(total, dtype=I32))
    number = jnp.arange(total, dtype=I32)
    last = jnp.maximum(count - 1, 0)
    tail_tile = jnp.sum(jnp.where(number == last, tiles, 0))
    tail_slot = jnp.sum(jnp.where(number == last, slots, 0))
    tiles = jnp.where(number < count, tiles, tail_tile)
    slots = jnp.where(number < count, slots, tail_slot)
    return jnp.concatenate([tiles, slots, count[None]])


def add_children(table, base, arrived):
    total = arrived.shape[0]

    def tile_spec():
        return pl.BlockSpec((BLK, BLK), lambda n, t: (t[n] // 4, t[n] % 4))

    return pl.pallas_call(
        add_kernel,
        out_shape=jax.ShapeDtypeStruct(base.shape, F32),
        grid_spec=pltpu.PrefetchScalarGridSpec(
            num_scalar_prefetch=1,
            grid=(total,),
            in_specs=[tile_spec(), pl.BlockSpec((1, BLK, BLK), lambda n, t: (t[32 + n], 0, 0))],
            out_specs=tile_spec(),
        ),
        input_output_aliases={1: 0},
        cost_estimate=pl.CostEstimate(flops=4_000_000, bytes_accessed=24 << 20, transcendentals=0),
        name="add_children",
    )(table, base, arrived)


def on_device(front_matrix, child_blocks, child_target, child_place, child_live):
    mesh_rows = lax.axis_size("row")
    mesh_cols = lax.axis_size("col")
    row = lax.axis_index("row")
    column = lax.axis_index("col")
    x, y, z, core = column // SIDE, column % SIDE, row // 2, row % 2
    slab = front_matrix[:, :BLK]

    own, other = gather_lead(slab[:BLK], x, z)
    ta, tb = gather_rows(slab, x)
    uc = gather_cols(slab)

    packed = map_children(child_blocks, child_target, child_place, child_live, mesh_cols)
    arrived = lax.all_to_all(
        packed.reshape(mesh_cols, CAP, BLK, BLK), "col", split_axis=0, concat_axis=0, tiled=True
    ).reshape(mesh_cols * CAP, BLK, BLK)
    targets = lax.all_gather(child_target, "col", axis=0, tiled=False)
    arrivals = add_table(targets, mesh_rows, mesh_cols, column)

    four = jnp.arange(SIDE, dtype=I32)
    at_x = ring_place(four - x)[:, None]
    at_y = ring_place(four - y)[None, :]
    by_y = (at_y * SIDE + at_x).reshape(-1)
    by_x = (at_x * SIDE + at_y).reshape(-1)
    at_z = ring_place(four - z)[None, :]
    pick = jnp.where(four // 2 == core, 0, 8)[:, None]
    by_z = (pick + at_z * 2 + (four % 2)[:, None]).reshape(-1)

    lead_table = jnp.concatenate([by_y, 16 + by_x, core[None]]).astype(I32)
    factor, inverse = factor_lead(lead_table, own, other)
    table = jnp.concatenate([by_y, by_x, by_z, row[None], column[None]]).astype(I32)
    base = update_front(table, uc, ta, tb, front_matrix, factor, inverse)
    return add_children(arrivals, base, arrived)


def solution(mesh):
    return jax.shard_map(
        on_device,
        mesh=mesh,
        in_specs=(
            P("row", "col"),
            P(("row", "col"), None, None),
            P(("row", "col"), None),
            P(("row", "col"), None, None),
            P(("row", "col"), None),
        ),
        out_specs=P("row", "col"),
        check_vma=False,
    )
```

```python
import functools

import jax
import jax.numpy as jnp
from jax import lax
from jax.experimental import pallas as pl
from jax.experimental.pallas import tpu as pltpu
from jax.sharding import PartitionSpec as P

F32 = jnp.float32
BF16 = jnp.bfloat16
I32 = jnp.int32
BLK = 256
LEADS = 4
CAP = 2
SIDE = 4
NB = 128
HIGHEST = lax.Precision.HIGHEST


def dot_nt(left, right, precision=None):
    return lax.dot_general(
        left, right, (((1,), (1,)), ((), ())), precision=precision, preferred_element_type=F32
    )


def dot_nn(left, right, precision=None):
    return lax.dot_general(
        left, right, (((1,), (0,)), ((), ())), precision=precision, preferred_element_type=F32
    )


def split2(value):
    high = value.astype(BF16)
    return high, (value - high.astype(F32)).astype(BF16)


def swap_cores(value):
    return lax.ppermute(value, "row", [(r, r ^ 1) for r in range(8)])


def spread_x(parts, x):
    out = jnp.where(x == 0, parts[0], jnp.zeros_like(parts[0]))
    for q in range(1, SIDE):
        out = out + lax.ppermute(parts[q], "col", [(y, q * SIDE + y) for y in range(SIDE)])
    return out


def after(value, *earlier):
    return lax.optimization_barrier((value,) + earlier)[0]


def exchange(value, axis):
    return lax.all_to_all(value, axis, split_axis=0, concat_axis=0, tiled=True)


def to_all(value, axis):
    copies = lax.axis_size(axis)
    return exchange(jnp.broadcast_to(value[None], (copies,) + value.shape), axis)


LOWER = (((0, 0), (1, 0), (2, 0), (3, 0), (1, 1)), ((2, 1), (3, 1), (2, 2), (3, 2), (3, 3)))


def lead_share(strip, core):
    four = to_all(strip, "row")[:LEADS]
    first, second = [jnp.concatenate([four[i, j] for i, j in half], axis=0) for half in LOWER]
    return jnp.where(core == 0, first, second), four


def col_pieces(slab):
    blocks = slab.reshape(8, BLK, BLK)
    out = None
    for h in range(2):
        for q in range(2):
            pairs = []
            for r in range(8):
                for j in range(LEADS):
                    pairs.append((r * 16 + j, (2 * j + q) * 16 + r + 8 * h))
            part = jnp.stack([blocks[4 * q + h], blocks[4 * q + 2 + h]])
            part = lax.ppermute(part, ("row", "col"), pairs)
            out = part if out is None else out + part
    return out


def factor_block(a, u_ref, e_ref):
    n = a.shape[0]
    ri = lax.broadcasted_iota(I32, (n, n), 0)
    ci = lax.broadcasted_iota(I32, (n, n), 1)
    e = jnp.where(ri == ci, F32(1), F32(0))
    base = 0
    for p in range(0, n, 4):
        off = p - base
        m = a.shape[0]
        cols = [jnp.broadcast_to(a[:, p + v : p + v + 1], (m, n)) for v in range(4)]
        s = [[cols[v][off + i : off + i + 1, :] for v in range(4)] for i in range(4)]
        arow = [a[off + i : off + i + 1, :] for i in range(4)]
        erow = [e[off + i : off + i + 1, :] for i in range(4)]
        inverse = []
        for q in range(4):
            r = F32(1) / s[q][q]
            inverse.append(r)
            low = [None] * 4
            for i in range(q + 1, 4):
                low[i] = s[i][q] * r
            for i in range(q + 1, 4):
                for v in range(q + 1, i + 1):
                    s[i][v] = s[i][v] - low[i] * s[v][q]
                arow[i] = arow[i] - low[i] * arow[q]
                erow[i] = erow[i] - low[i] * erow[q]
        for q in range(4):
            scale = lax.rsqrt(s[q][q])
            u_ref[p + q : p + q + 1, :] = arow[q] * scale
            e_ref[p + q : p + q + 1, :] = erow[q] * scale
        following = p + 4
        if following >= n:
            break
        live = None
        if following % 8 == 0:
            cut = following - base
            a, e, cols = a[cut:], e[cut:], [c[cut:] for c in cols]
            base = following
        else:
            live = lax.broadcasted_iota(I32, a.shape, 0) >= following - base
        times = []
        for q in range(4):
            c = cols[q]
            for v in range(q):
                c = c - times[v] * s[q][v]
            times.append(c * inverse[q])
        da = times[0] * arow[0]
        de = times[0] * erow[0]
        for q in range(1, 4):
            da = da + times[q] * arow[q]
            de = de + times[q] * erow[q]
        if live is not None:
            da = jnp.where(live, da, F32(0))
            de = jnp.where(live, de, F32(0))
        a = a - da
        e = e - de


def factor_kernel(table, own_ref, other_ref, l_ref, high_ref, low_ref, m_ref, inv_ref, u_ref, e_ref):
    n = m_ref.shape[0]
    steps = n // NB
    strips = own_ref.shape[0]
    tall = BLK // strips

    def assemble(sources):
        def place(number, carry):
            for half, source in zip(LOWER, sources):
                for spot, (i, j) in enumerate(half):
                    row = pl.multiple_of(i * BLK + number * tall, tall)
                    m_ref[pl.ds(row, tall), j * BLK : (j + 1) * BLK] = source[
                        number, spot * tall : (spot + 1) * tall, :
                    ]
            return carry

        lax.fori_loop(0, strips, place, 0)

    @pl.when(table[0] == 0)
    def _():
        assemble((own_ref, other_ref))

    @pl.when(table[0] != 0)
    def _():
        assemble((other_ref, own_ref))

    l_ref[...] = jnp.zeros_like(l_ref)
    inv_ref[...] = jnp.zeros_like(inv_ref)
    ri = lax.broadcasted_iota(I32, (NB, NB), 0)
    ci = lax.broadcasted_iota(I32, (NB, NB), 1)

    def step(k, carry):
        at = pl.multiple_of(k * NB, NB)
        d = m_ref[pl.ds(at, NB), pl.ds(at, NB)]
        factor_block(jnp.where(ri >= ci, d, d.T), u_ref, e_ref)
        l_ref[pl.ds(at, NB), pl.ds(at, NB)] = jnp.where(ri <= ci, u_ref[...], F32(0)).T
        ik = jnp.where(ri >= ci, e_ref[...], F32(0))
        for kk in range(steps):

            @pl.when(k == kk)
            def _():
                lo, hi = kk * NB, (kk + 1) * NB
                if kk < steps - 1:
                    panel = dot_nt(m_ref[hi:, lo:hi], ik, HIGHEST)
                    l_ref[hi:, lo:hi] = panel
                    m_ref[hi:, hi:] = m_ref[hi:, hi:] - dot_nt(panel, panel, HIGHEST)
                if kk > 0:
                    inv_ref[lo:hi, :lo] = dot_nn(ik, inv_ref[lo:hi, :lo], HIGHEST)
                inv_ref[lo:hi, lo:hi] = ik
                if kk < steps - 1:
                    inv_ref[hi:, :hi] = inv_ref[hi:, :hi] - dot_nn(
                        panel, inv_ref[lo:hi, :hi], HIGHEST
                    )

        return carry

    lax.fori_loop(0, steps, step, 0)
    for i in range(LEADS):
        rows = slice(i * BLK, (i + 1) * BLK)
        high_ref[rows, :], low_ref[rows, :] = split2(inv_ref[rows, :])


def factor_lead(table, *parts):
    n = LEADS * BLK
    vmem = pl.BlockSpec(memory_space=pltpu.VMEM)
    return pl.pallas_call(
        factor_kernel,
        out_shape=(
            jax.ShapeDtypeStruct((n, n), F32),
            jax.ShapeDtypeStruct((n, n), BF16),
            jax.ShapeDtypeStruct((n, n), BF16),
        ),
        in_specs=[pl.BlockSpec(memory_space=pltpu.SMEM)] + [vmem] * 2,
        out_specs=[vmem, vmem, vmem],
        scratch_shapes=[
            pltpu.VMEM((n, n), F32),
            pltpu.VMEM((n, n), F32),
            pltpu.VMEM((NB, NB), F32),
            pltpu.VMEM((NB, NB), F32),
        ],
        compiler_params=pltpu.CompilerParams(vmem_limit_bytes=40 << 20),
        cost_estimate=pl.CostEstimate(flops=60_000_000_000, bytes_accessed=10 << 20, transcendentals=0),
        name="factor_lead",
    )(table, *parts)


def update_kernel(table, *refs):
    uc, raw = refs[0:4], refs[4:8]
    front_ref, own_ref, high_ref, low_ref, out_ref = refs[8:13]
    ch, cl, rh, rl, pan = refs[13:]
    g = pl.program_id(0)
    r, c = table[0], table[1]

    upper, lower = slice(0, BLK), slice(BLK, 2 * BLK)

    def solve():
        high, low = rh[...], rl[...]
        out = []
        for j in range(LEADS):
            hi = (j + 1) * BLK
            rows = slice(j * BLK, hi)
            out.append(
                dot_nt(high[:, :hi], high_ref[rows, :hi])
                + (
                    dot_nt(high[:, :hi], low_ref[rows, :hi])
                    + dot_nt(low[:, :hi], high_ref[rows, :hi])
                )
            )
        return out

    @pl.when(g < 2)
    def _():
        for j in range(LEADS):
            cols = slice(j * BLK, (j + 1) * BLK)
            rh[upper, cols], rl[upper, cols] = split2(uc[j][0, 0])
            rh[lower, cols], rl[lower, cols] = split2(uc[j][0, 1])
        got = solve()
        at = pl.ds(pl.multiple_of(g * 2 * BLK, BLK), 2 * BLK)
        for j in range(LEADS):
            cols = slice(j * BLK, (j + 1) * BLK)
            ch[at, cols], cl[at, cols] = split2(got[j])

    @pl.when(g >= 2)
    def _():
        for j in range(LEADS):
            cols = slice(j * BLK, (j + 1) * BLK)
            rh[:, cols], rl[:, cols] = split2(raw[j][0])
        got = solve()
        special = (g == 2) & (r < LEADS)
        top = lax.broadcasted_iota(I32, (2 * BLK, BLK), 0) < BLK
        left = []
        for j in range(LEADS):
            cols = slice(j * BLK, (j + 1) * BLK)
            own = own_ref[:, cols]
            own = jnp.concatenate([own, own], axis=0)
            keep = jnp.where((r >= 2) & (j < 2), F32(1), F32(0))
            left.append(jnp.where(top & special, own * keep, got[j]))

            @pl.when(c == j)
            def _():
                pan[...] = jnp.where(top & special, own, got[j])

        left_h, left_l = split2(jnp.concatenate(left, axis=1))
        for t in range(4):
            rows = slice(t * BLK, (t + 1) * BLK)
            right_h, right_l = ch[rows, :], cl[rows, :]
            out_ref[:, rows] = front_ref[:, rows] - (
                dot_nt(left_h, right_h) + (dot_nt(left_h, right_l) + dot_nt(left_l, right_h))
            )

        @pl.when(c < LEADS)
        def _():
            out_ref[:, :BLK] = pan[...]


def update_front(table, uc, raw, front, factor, high, low):
    n = LEADS * BLK
    rows, cols = front.shape
    tall = 2 * BLK

    def step(g):
        return jnp.maximum(g - 2, 0)

    def tall_spec():
        return pl.BlockSpec((tall, cols), lambda g, t: (step(g), 0))

    def raw_spec(j):
        return pl.BlockSpec((1, tall, BLK), lambda g, t: (step(g) * SIDE + j, 0, 0))

    def uc_spec(j):
        return pl.BlockSpec((1, 2, BLK, BLK), lambda g, t: (2 * j + jnp.minimum(g, 1), 0, 0, 0))

    in_specs = [uc_spec(j) for j in range(LEADS)]
    in_specs += [raw_spec(j) for j in range(LEADS)]
    in_specs += [
        tall_spec(),
        pl.BlockSpec((BLK, n), lambda g, t: (jnp.minimum(t[0], LEADS - 1), 0)),
        pl.BlockSpec((n, n), lambda g, t: (0, 0)),
        pl.BlockSpec((n, n), lambda g, t: (0, 0)),
    ]
    return pl.pallas_call(
        update_kernel,
        out_shape=jax.ShapeDtypeStruct((rows, cols), F32),
        grid_spec=pltpu.PrefetchScalarGridSpec(
            num_scalar_prefetch=1,
            grid=(2 + rows // tall,),
            in_specs=in_specs,
            out_specs=tall_spec(),
            scratch_shapes=[
                pltpu.VMEM((n, n), BF16),
                pltpu.VMEM((n, n), BF16),
                pltpu.VMEM((tall, n), BF16),
                pltpu.VMEM((tall, n), BF16),
                pltpu.VMEM((tall, BLK), F32),
            ],
        ),
        compiler_params=pltpu.CompilerParams(vmem_limit_bytes=58 << 20),
        cost_estimate=pl.CostEstimate(flops=26_000_000_000, bytes_accessed=36 << 20, transcendentals=0),
        name="update_front",
    )(table, *([uc] * LEADS), *([raw] * LEADS), front, factor, high, low)


def slots_of(target, mesh_cols):
    kids = target.shape[-2]
    same = jnp.all(target[..., :, None, :] == target[..., None, :, :], axis=-1)
    number = jnp.arange(kids, dtype=I32)
    first = jnp.min(jnp.where(same, number, kids), axis=-1)
    leads = first == number
    goal = target[..., 1] % mesh_cols
    alike = (goal[..., :, None] == goal[..., None, :]) & leads[..., None, :]
    rank = jnp.sum((alike & (number < first[..., :, None])).astype(I32), axis=-1)
    return goal * CAP + rank, leads


def sort_order(keys):
    count = keys.shape[0]
    number = jnp.arange(count, dtype=I32)
    before = (keys[None, :] < keys[:, None]) | (
        (keys[None, :] == keys[:, None]) & (number[None, :] < number[:, None])
    )
    place = jnp.sum(before.astype(I32), axis=1)
    hot = (place[None, :] == number[:, None]).astype(I32)
    return lambda values: jnp.sum(hot * values[None, :], axis=1)


def map_kernel(table, block_ref, place_ref, out_ref):
    k = pl.program_id(0)
    live_row, live_col = table[16 + k], table[24 + k]
    target = lax.broadcasted_iota(I32, (BLK, BLK), 0)
    source = lax.broadcasted_iota(I32, (BLK, BLK), 1)

    def picks(index, live):
        hit = (place_ref[0, index : index + 1, :] == target) & (source < live)
        return jnp.where(hit, F32(1), F32(0)).astype(BF16)

    def parts(value):
        high = value.astype(BF16)
        rest = value - high.astype(F32)
        middle = rest.astype(BF16)
        return high, middle, (rest - middle.astype(F32)).astype(BF16)

    row_pick, col_pick = picks(0, live_row), picks(1, live_col)
    high, middle, low = parts(block_ref[0])
    moved = dot_nn(row_pick, high) + (dot_nn(row_pick, middle) + dot_nn(row_pick, low))
    high, middle, low = parts(moved)
    mapped = dot_nt(high, col_pick) + (dot_nt(middle, col_pick) + dot_nt(low, col_pick))
    opens = (k == 0) | (table[8 + k] != table[8 + jnp.maximum(k - 1, 0)])

    @pl.when(opens)
    def _():
        out_ref[0] = mapped

    @pl.when(jnp.logical_not(opens))
    def _():
        out_ref[0] = out_ref[0] + mapped


def map_children(child_blocks, child_target, child_place, child_live, mesh_cols):
    kids = child_blocks.shape[0]
    slot, _ = slots_of(child_target, mesh_cols)
    ordered = sort_order(slot)
    table = jnp.concatenate(
        [
            ordered(jnp.arange(kids, dtype=I32)),
            ordered(slot),
            ordered(child_live[:, 0]),
            ordered(child_live[:, 1]),
        ]
    )
    return pl.pallas_call(
        map_kernel,
        out_shape=jax.ShapeDtypeStruct((mesh_cols * CAP, BLK, BLK), F32),
        grid_spec=pltpu.PrefetchScalarGridSpec(
            num_scalar_prefetch=1,
            grid=(kids,),
            in_specs=[
                pl.BlockSpec((1, BLK, BLK), lambda k, t: (t[k], 0, 0)),
                pl.BlockSpec((1, 2, BLK), lambda k, t: (t[k], 0, 0)),
            ],
            out_specs=pl.BlockSpec((1, BLK, BLK), lambda k, t: (t[8 + k], 0, 0)),
        ),
        cost_estimate=pl.CostEstimate(flops=2_000_000_000, bytes_accessed=4 << 20, transcendentals=0),
        name="map_children",
    )(table, child_blocks, child_place)


def add_kernel(table, base_ref, slot_ref, out_ref, buffers, sems, next_ref):
    row = pl.program_id(0)
    total = 32
    count = table[2 * total]
    deep = buffers.shape[0]

    def copy(n):
        k = lax.rem(n, deep)
        return pltpu.make_async_copy(slot_ref.at[table[total + n]], buffers.at[k], sems.at[k])

    @pl.when(row == 0)
    def _():
        next_ref[0] = 0
        for n in range(deep):

            @pl.when(n < count)
            def _():
                copy(jnp.int32(n)).start()

    out_ref[...] = base_ref[...]

    def here(n):
        return (n < count) & (lax.div(table[jnp.minimum(n, total - 1)], 4) == row)

    def add(n):
        copy(n).wait()
        cols = pl.ds(pl.multiple_of(lax.rem(table[n], 4) * BLK, BLK), BLK)
        out_ref[:, cols] = out_ref[:, cols] + buffers[lax.rem(n, deep)]

        @pl.when(n + deep < count)
        def _():
            copy(n + deep).start()

        return n + 1

    next_ref[0] = lax.while_loop(here, add, next_ref[0])


def add_table_kernel(mesh_rows, mesh_cols, kids, info_ref, notes_ref, out_ref, head, link):
    total = mesh_cols * CAP
    column = info_ref[0]

    def clear(n, carry):
        head[n] = -1
        return carry

    lax.fori_loop(0, 32, clear, 0)

    def source(s, carry):

        def child(k, found):
            count, old, seen = found
            down, across = notes_ref[s, 2 * k], notes_ref[s, 2 * k + 1]
            tile = lax.div(down, mesh_rows) * 4 + lax.div(across, mesh_cols)
            fresh = (lax.rem(across, mesh_cols) == column) & (tile != old) & (tile != seen)

            @pl.when(fresh)
            def _():
                link[s * CAP + count] = head[tile]
                head[tile] = s * CAP + count

            return (
                jnp.where(fresh, count + 1, count),
                jnp.where(fresh, seen, old),
                jnp.where(fresh, tile, seen),
            )

        lax.fori_loop(0, kids, child, (jnp.int32(0), jnp.int32(-1), jnp.int32(-1)))
        return carry

    lax.fori_loop(0, mesh_cols, source, 0)

    def walk(tile, n):
        def one(state):
            n, slot = state
            out_ref[n] = tile
            out_ref[total + n] = slot
            return n + 1, link[slot]

        return lax.while_loop(lambda state: state[1] >= 0, one, (n, head[tile]))[0]

    count = lax.fori_loop(0, 32, walk, jnp.int32(0))
    out_ref[2 * total] = count

    def fill(n, carry):
        last = jnp.maximum(count - 1, 0)
        none = count == 0
        out_ref[n] = jnp.where(none, 0, out_ref[last])
        out_ref[total + n] = jnp.where(none, 0, out_ref[total + last])
        return carry

    lax.fori_loop(count, total, fill, 0)


def add_table(info, notes, mesh_rows, mesh_cols, kids):
    smem = pl.BlockSpec(memory_space=pltpu.SMEM)
    total = mesh_cols * CAP
    return pl.pallas_call(
        functools.partial(add_table_kernel, mesh_rows, mesh_cols, kids),
        out_shape=jax.ShapeDtypeStruct((2 * total + 1,), I32),
        in_specs=[smem, smem],
        out_specs=smem,
        scratch_shapes=[pltpu.SMEM((32,), I32), pltpu.SMEM((total,), I32)],
        name="add_table",
    )(info, notes)


def add_children(table, base, arrived):
    rows, cols = base.shape
    deep = 8

    def row_spec():
        return pl.BlockSpec((BLK, cols), lambda n, t: (n, 0))

    return pl.pallas_call(
        add_kernel,
        out_shape=jax.ShapeDtypeStruct(base.shape, F32),
        grid_spec=pltpu.PrefetchScalarGridSpec(
            num_scalar_prefetch=1,
            grid=(rows // BLK,),
            in_specs=[row_spec(), pl.BlockSpec(memory_space=pl.ANY)],
            out_specs=row_spec(),
            scratch_shapes=[
                pltpu.VMEM((deep, BLK, BLK), F32),
                pltpu.SemaphoreType.DMA((deep,)),
                pltpu.SMEM((1,), I32),
            ],
        ),
        input_output_aliases={1: 0},
        compiler_params=pltpu.CompilerParams(vmem_limit_bytes=32 << 20),
        cost_estimate=pl.CostEstimate(flops=4_000_000, bytes_accessed=24 << 20, transcendentals=0),
        name="add_children",
    )(table, base, arrived)


def on_device(front_matrix, child_blocks, child_target, child_place, child_live):
    mesh_rows = lax.axis_size("row")
    mesh_cols = lax.axis_size("col")
    row = lax.axis_index("row")
    column = lax.axis_index("col")
    x, core = column // SIDE, row % 2
    slab = front_matrix[:, :BLK]

    table = jnp.stack([row, column]).astype(I32)

    strip = exchange(slab[:BLK].reshape(mesh_cols, -1, BLK), "col")[:LEADS]
    late = after(slab, strip)
    rows = slab.shape[0] // SIDE
    piece = spread_x([late[q * rows : (q + 1) * rows] for q in range(SIDE)], x)
    uc = col_pieces(late)
    share, four = lead_share(strip, core)
    raw = lax.all_gather(after(piece, four), "col", axis=0, tiled=False)
    packed = map_children(child_blocks, child_target, child_place, child_live, mesh_cols)

    note = jnp.zeros((8, BLK), F32)
    note = note.at[0, : child_target.size].set(child_target.reshape(-1).astype(F32))
    share, packed, uc = lax.optimization_barrier(
        (jnp.concatenate([share, note], axis=0), packed, uc)
    )
    uc = lax.all_gather(uc, "row", axis=0, tiled=False)
    own = to_all(share, "col")
    packed = after(packed, own)
    arrived = exchange(packed.reshape(mesh_cols, CAP, BLK, BLK), "col")
    arrived = arrived.reshape(mesh_cols * CAP, BLK, BLK)
    other = swap_cores(own)

    factor, high, low = factor_lead(core[None].astype(I32), own, other)
    base = update_front(table, uc, raw, front_matrix, factor, high, low)
    notes = after(own, base)[:, -8, : child_target.size].astype(I32)
    arrivals = add_table(column[None].astype(I32), notes, mesh_rows, mesh_cols, child_target.shape[0])
    return add_children(arrivals, base, arrived)


def solution(mesh):
    return jax.shard_map(
        on_device,
        mesh=mesh,
        in_specs=(
            P("row", "col"),
            P(("row", "col"), None, None),
            P(("row", "col"), None),
            P(("row", "col"), None, None),
            P(("row", "col"), None),
        ),
        out_specs=P("row", "col"),
        check_vma=False,
    )
```

```python
import functools

import jax
import jax.numpy as jnp
from jax import lax
from jax.experimental import pallas as pl
from jax.experimental.pallas import tpu as pltpu
from jax.sharding import PartitionSpec as P

F32 = jnp.float32
BF16 = jnp.bfloat16
I32 = jnp.int32
BLK = 256
LEADS = 4
CAP = 2
SIDE = 4
NB = 128
HIGHEST = lax.Precision.HIGHEST


def dot_nt(left, right, precision=None):
    return lax.dot_general(
        left, right, (((1,), (1,)), ((), ())), precision=precision, preferred_element_type=F32
    )


def dot_nn(left, right, precision=None):
    return lax.dot_general(
        left, right, (((1,), (0,)), ((), ())), precision=precision, preferred_element_type=F32
    )


def split2(value):
    high = value.astype(BF16)
    return high, (value - high.astype(F32)).astype(BF16)


def swap_cores(value):
    return lax.ppermute(value, "row", [(r, r ^ 1) for r in range(8)])


def spread_x(parts, x):
    out = jnp.where(x == 0, parts[0], jnp.zeros_like(parts[0]))
    for q in range(1, SIDE):
        out = out + lax.ppermute(parts[q], "col", [(y, q * SIDE + y) for y in range(SIDE)])
    return out


def after(value, *earlier):
    return lax.optimization_barrier((value,) + earlier)[0]


def exchange(value, axis):
    return lax.all_to_all(value, axis, split_axis=0, concat_axis=0, tiled=True)


def to_all(value, axis):
    copies = lax.axis_size(axis)
    return exchange(jnp.broadcast_to(value[None], (copies,) + value.shape), axis)


LOWER = (((0, 0), (1, 0), (2, 0), (3, 0), (1, 1)), ((2, 1), (3, 1), (2, 2), (3, 2), (3, 3)))


def lead_share(strip, core):
    four = to_all(strip, "row")[:LEADS]
    first, second = [jnp.concatenate([four[i, j] for i, j in half], axis=0) for half in LOWER]
    return jnp.where(core == 0, first, second), four


def col_pieces(slab):
    blocks = slab.reshape(8, BLK, BLK)
    out = None
    for h in range(2):
        for q in range(2):
            pairs = []
            for r in range(8):
                for j in range(LEADS):
                    pairs.append((r * 16 + j, (2 * j + q) * 16 + r + 8 * h))
            part = jnp.stack([blocks[4 * q + h], blocks[4 * q + 2 + h]])
            part = lax.ppermute(part, ("row", "col"), pairs)
            out = part if out is None else out + part
    return out


def factor_block(a, u_ref, e_ref):
    n = a.shape[0]
    ri = lax.broadcasted_iota(I32, (n, n), 0)
    ci = lax.broadcasted_iota(I32, (n, n), 1)
    e = jnp.where(ri == ci, F32(1), F32(0))
    base = 0
    for p in range(0, n, 4):
        off = p - base
        m = a.shape[0]
        cols = [jnp.broadcast_to(a[:, p + v : p + v + 1], (m, n)) for v in range(4)]
        s = [[cols[v][off + i : off + i + 1, :] for v in range(4)] for i in range(4)]
        arow = [a[off + i : off + i + 1, :] for i in range(4)]
        erow = [e[off + i : off + i + 1, :] for i in range(4)]
        inverse = []
        for q in range(4):
            r = F32(1) / s[q][q]
            inverse.append(r)
            low = [None] * 4
            for i in range(q + 1, 4):
                low[i] = s[i][q] * r
            for i in range(q + 1, 4):
                for v in range(q + 1, i + 1):
                    s[i][v] = s[i][v] - low[i] * s[v][q]
                arow[i] = arow[i] - low[i] * arow[q]
                erow[i] = erow[i] - low[i] * erow[q]
        for q in range(4):
            scale = lax.rsqrt(s[q][q])
            u_ref[p + q : p + q + 1, :] = arow[q] * scale
            e_ref[p + q : p + q + 1, :] = erow[q] * scale
        following = p + 4
        if following >= n:
            break
        live = None
        if following % 8 == 0:
            cut = following - base
            a, e, cols = a[cut:], e[cut:], [c[cut:] for c in cols]
            base = following
        else:
            live = lax.broadcasted_iota(I32, a.shape, 0) >= following - base
        times = []
        for q in range(4):
            c = cols[q]
            for v in range(q):
                c = c - times[v] * s[q][v]
            times.append(c * inverse[q])
        da = times[0] * arow[0]
        de = times[0] * erow[0]
        for q in range(1, 4):
            da = da + times[q] * arow[q]
            de = de + times[q] * erow[q]
        if live is not None:
            da = jnp.where(live, da, F32(0))
            de = jnp.where(live, de, F32(0))
        a = a - da
        e = e - de


def factor_kernel(table, own_ref, other_ref, l_ref, high_ref, low_ref, m_ref, inv_ref, u_ref, e_ref):
    n = m_ref.shape[0]
    steps = n // NB
    strips = own_ref.shape[0]
    tall = BLK // strips

    def assemble(sources):
        def place(number, carry):
            for half, source in zip(LOWER, sources):
                for spot, (i, j) in enumerate(half):
                    row = pl.multiple_of(i * BLK + number * tall, tall)
                    m_ref[pl.ds(row, tall), j * BLK : (j + 1) * BLK] = source[
                        number, spot * tall : (spot + 1) * tall, :
                    ]
            return carry

        lax.fori_loop(0, strips, place, 0)

    @pl.when(table[0] == 0)
    def _():
        assemble((own_ref, other_ref))

    @pl.when(table[0] != 0)
    def _():
        assemble((other_ref, own_ref))

    l_ref[...] = jnp.zeros_like(l_ref)
    inv_ref[...] = jnp.zeros_like(inv_ref)
    ri = lax.broadcasted_iota(I32, (NB, NB), 0)
    ci = lax.broadcasted_iota(I32, (NB, NB), 1)

    def step(k, carry):
        at = pl.multiple_of(k * NB, NB)
        d = m_ref[pl.ds(at, NB), pl.ds(at, NB)]
        factor_block(jnp.where(ri >= ci, d, d.T), u_ref, e_ref)
        l_ref[pl.ds(at, NB), pl.ds(at, NB)] = jnp.where(ri <= ci, u_ref[...], F32(0)).T
        ik = jnp.where(ri >= ci, e_ref[...], F32(0))
        for kk in range(steps):

            @pl.when(k == kk)
            def _():
                lo, hi = kk * NB, (kk + 1) * NB
                if kk < steps - 1:
                    panel = dot_nt(m_ref[hi:, lo:hi], ik, HIGHEST)
                    l_ref[hi:, lo:hi] = panel
                    m_ref[hi:, hi:] = m_ref[hi:, hi:] - dot_nt(panel, panel, HIGHEST)
                if kk > 0:
                    inv_ref[lo:hi, :lo] = dot_nn(ik, inv_ref[lo:hi, :lo], HIGHEST)
                inv_ref[lo:hi, lo:hi] = ik
                if kk < steps - 1:
                    inv_ref[hi:, :hi] = inv_ref[hi:, :hi] - dot_nn(
                        panel, inv_ref[lo:hi, :hi], HIGHEST
                    )

        return carry

    lax.fori_loop(0, steps, step, 0)
    for i in range(LEADS):
        rows = slice(i * BLK, (i + 1) * BLK)
        high_ref[rows, :], low_ref[rows, :] = split2(inv_ref[rows, :])


def factor_lead(table, *parts):
    n = LEADS * BLK
    vmem = pl.BlockSpec(memory_space=pltpu.VMEM)
    return pl.pallas_call(
        factor_kernel,
        out_shape=(
            jax.ShapeDtypeStruct((n, n), F32),
            jax.ShapeDtypeStruct((n, n), BF16),
            jax.ShapeDtypeStruct((n, n), BF16),
        ),
        in_specs=[pl.BlockSpec(memory_space=pltpu.SMEM)] + [vmem] * 2,
        out_specs=[vmem, vmem, vmem],
        scratch_shapes=[
            pltpu.VMEM((n, n), F32),
            pltpu.VMEM((n, n), F32),
            pltpu.VMEM((NB, NB), F32),
            pltpu.VMEM((NB, NB), F32),
        ],
        compiler_params=pltpu.CompilerParams(vmem_limit_bytes=40 << 20),
        cost_estimate=pl.CostEstimate(flops=60_000_000_000, bytes_accessed=10 << 20, transcendentals=0),
        name="factor_lead",
    )(table, *parts)


def update_kernel(table, *refs):
    uc, raw = refs[0:4], refs[4:8]
    front_ref, own_ref, high_ref, low_ref, out_ref = refs[8:13]
    ch, cl, rh, rl, pan = refs[13:]
    g = pl.program_id(0)
    r, c = table[0], table[1]

    upper, lower = slice(0, BLK), slice(BLK, 2 * BLK)

    def solve():
        high, low = rh[...], rl[...]
        out = []
        for j in range(LEADS):
            hi = (j + 1) * BLK
            rows = slice(j * BLK, hi)
            out.append(
                dot_nt(high[:, :hi], high_ref[rows, :hi])
                + (
                    dot_nt(high[:, :hi], low_ref[rows, :hi])
                    + dot_nt(low[:, :hi], high_ref[rows, :hi])
                )
            )
        return out

    @pl.when(g < 2)
    def _():
        for j in range(LEADS):
            cols = slice(j * BLK, (j + 1) * BLK)
            rh[upper, cols], rl[upper, cols] = split2(uc[j][0, 0])
            rh[lower, cols], rl[lower, cols] = split2(uc[j][0, 1])
        got = solve()
        at = pl.ds(pl.multiple_of(g * 2 * BLK, BLK), 2 * BLK)
        for j in range(LEADS):
            cols = slice(j * BLK, (j + 1) * BLK)
            ch[at, cols], cl[at, cols] = split2(got[j])

    @pl.when(g >= 2)
    def _():
        for j in range(LEADS):
            cols = slice(j * BLK, (j + 1) * BLK)
            rh[:, cols], rl[:, cols] = split2(raw[j][0])
        got = solve()
        special = (g == 2) & (r < LEADS)
        top = lax.broadcasted_iota(I32, (2 * BLK, BLK), 0) < BLK
        left = []
        for j in range(LEADS):
            cols = slice(j * BLK, (j + 1) * BLK)
            own = own_ref[:, cols]
            own = jnp.concatenate([own, own], axis=0)
            keep = jnp.where((r >= 2) & (j < 2), F32(1), F32(0))
            left.append(jnp.where(top & special, own * keep, got[j]))

            @pl.when(c == j)
            def _():
                pan[...] = jnp.where(top & special, own, got[j])

        left_h, left_l = split2(jnp.concatenate(left, axis=1))
        for t in range(4):
            rows = slice(t * BLK, (t + 1) * BLK)
            right_h, right_l = ch[rows, :], cl[rows, :]
            out_ref[:, rows] = front_ref[:, rows] - (
                dot_nt(left_h, right_h) + (dot_nt(left_h, right_l) + dot_nt(left_l, right_h))
            )

        @pl.when(c < LEADS)
        def _():
            out_ref[:, :BLK] = pan[...]


def update_front(table, uc, raw, front, factor, high, low):
    n = LEADS * BLK
    rows, cols = front.shape
    tall = 2 * BLK

    def step(g):
        return jnp.maximum(g - 2, 0)

    def tall_spec():
        return pl.BlockSpec((tall, cols), lambda g, t: (step(g), 0))

    def raw_spec(j):
        return pl.BlockSpec((1, tall, BLK), lambda g, t: (step(g) * SIDE + j, 0, 0))

    def uc_spec(j):
        return pl.BlockSpec((1, 2, BLK, BLK), lambda g, t: (2 * j + jnp.minimum(g, 1), 0, 0, 0))

    in_specs = [uc_spec(j) for j in range(LEADS)]
    in_specs += [raw_spec(j) for j in range(LEADS)]
    in_specs += [
        tall_spec(),
        pl.BlockSpec((BLK, n), lambda g, t: (jnp.minimum(t[0], LEADS - 1), 0)),
        pl.BlockSpec((n, n), lambda g, t: (0, 0)),
        pl.BlockSpec((n, n), lambda g, t: (0, 0)),
    ]
    return pl.pallas_call(
        update_kernel,
        out_shape=jax.ShapeDtypeStruct((rows, cols), F32),
        grid_spec=pltpu.PrefetchScalarGridSpec(
            num_scalar_prefetch=1,
            grid=(2 + rows // tall,),
            in_specs=in_specs,
            out_specs=tall_spec(),
            scratch_shapes=[
                pltpu.VMEM((n, n), BF16),
                pltpu.VMEM((n, n), BF16),
                pltpu.VMEM((tall, n), BF16),
                pltpu.VMEM((tall, n), BF16),
                pltpu.VMEM((tall, BLK), F32),
            ],
        ),
        compiler_params=pltpu.CompilerParams(vmem_limit_bytes=58 << 20),
        cost_estimate=pl.CostEstimate(flops=26_000_000_000, bytes_accessed=36 << 20, transcendentals=0),
        name="update_front",
    )(table, *([uc] * LEADS), *([raw] * LEADS), front, factor, high, low)


def slots_of(target, mesh_cols):
    kids = target.shape[-2]
    same = jnp.all(target[..., :, None, :] == target[..., None, :, :], axis=-1)
    number = jnp.arange(kids, dtype=I32)
    first = jnp.min(jnp.where(same, number, kids), axis=-1)
    leads = first == number
    goal = target[..., 1] % mesh_cols
    alike = (goal[..., :, None] == goal[..., None, :]) & leads[..., None, :]
    rank = jnp.sum((alike & (number < first[..., :, None])).astype(I32), axis=-1)
    return goal * CAP + rank, leads


def sort_order(keys):
    count = keys.shape[0]
    number = jnp.arange(count, dtype=I32)
    before = (keys[None, :] < keys[:, None]) | (
        (keys[None, :] == keys[:, None]) & (number[None, :] < number[:, None])
    )
    place = jnp.sum(before.astype(I32), axis=1)
    hot = (place[None, :] == number[:, None]).astype(I32)
    return lambda values: jnp.sum(hot * values[None, :], axis=1)


def map_kernel(table, block_ref, place_ref, out_ref):
    k = pl.program_id(0)
    live_row, live_col = table[16 + k], table[24 + k]
    target = lax.broadcasted_iota(I32, (BLK, BLK), 0)
    source = lax.broadcasted_iota(I32, (BLK, BLK), 1)

    def picks(index, live):
        hit = (place_ref[0, index : index + 1, :] == target) & (source < live)
        return jnp.where(hit, F32(1), F32(0)).astype(BF16)

    def parts(value):
        high = value.astype(BF16)
        rest = value - high.astype(F32)
        middle = rest.astype(BF16)
        return high, middle, (rest - middle.astype(F32)).astype(BF16)

    row_pick, col_pick = picks(0, live_row), picks(1, live_col)
    high, middle, low = parts(block_ref[0])
    moved = dot_nn(row_pick, high) + (dot_nn(row_pick, middle) + dot_nn(row_pick, low))
    high, middle, low = parts(moved)
    mapped = dot_nt(high, col_pick) + (dot_nt(middle, col_pick) + dot_nt(low, col_pick))
    opens = (k == 0) | (table[8 + k] != table[8 + jnp.maximum(k - 1, 0)])

    @pl.when(opens)
    def _():
        out_ref[0] = mapped

    @pl.when(jnp.logical_not(opens))
    def _():
        out_ref[0] = out_ref[0] + mapped


def map_children(child_blocks, child_target, child_place, child_live, mesh_cols):
    kids = child_blocks.shape[0]
    slot, _ = slots_of(child_target, mesh_cols)
    ordered = sort_order(slot)
    table = jnp.concatenate(
        [
            ordered(jnp.arange(kids, dtype=I32)),
            ordered(slot),
            ordered(child_live[:, 0]),
            ordered(child_live[:, 1]),
        ]
    )
    return pl.pallas_call(
        map_kernel,
        out_shape=jax.ShapeDtypeStruct((mesh_cols * CAP, BLK, BLK), F32),
        grid_spec=pltpu.PrefetchScalarGridSpec(
            num_scalar_prefetch=1,
            grid=(kids,),
            in_specs=[
                pl.BlockSpec((1, BLK, BLK), lambda k, t: (t[k], 0, 0)),
                pl.BlockSpec((1, 2, BLK), lambda k, t: (t[k], 0, 0)),
            ],
            out_specs=pl.BlockSpec((1, BLK, BLK), lambda k, t: (t[8 + k], 0, 0)),
        ),
        cost_estimate=pl.CostEstimate(flops=2_000_000_000, bytes_accessed=4 << 20, transcendentals=0),
        name="map_children",
    )(table, child_blocks, child_place)


def add_kernel(table, base_ref, slot_ref, out_ref, buffers, sems, next_ref):
    row = pl.program_id(0)
    total = 32
    count = table[2 * total]
    deep = buffers.shape[0]

    def copy(n):
        k = lax.rem(n, deep)
        return pltpu.make_async_copy(slot_ref.at[table[total + n]], buffers.at[k], sems.at[k])

    @pl.when(row == 0)
    def _():
        next_ref[0] = 0
        for n in range(deep):

            @pl.when(n < count)
            def _():
                copy(jnp.int32(n)).start()

    out_ref[...] = base_ref[...]

    def here(n):
        return (n < count) & (lax.div(table[jnp.minimum(n, total - 1)], 4) == row)

    def add(n):
        copy(n).wait()
        cols = pl.ds(pl.multiple_of(lax.rem(table[n], 4) * BLK, BLK), BLK)
        out_ref[:, cols] = out_ref[:, cols] + buffers[lax.rem(n, deep)]

        @pl.when(n + deep < count)
        def _():
            copy(n + deep).start()

        return n + 1

    next_ref[0] = lax.while_loop(here, add, next_ref[0])


def add_table_kernel(mesh_rows, mesh_cols, kids, info_ref, notes_ref, out_ref, head, link):
    total = mesh_cols * CAP
    column = info_ref[0]

    def clear(n, carry):
        head[n] = -1
        return carry

    lax.fori_loop(0, 32, clear, 0)

    def source(s, carry):

        def child(k, found):
            count, old, seen = found
            down, across = notes_ref[s, 2 * k], notes_ref[s, 2 * k + 1]
            tile = lax.div(down, mesh_rows) * 4 + lax.div(across, mesh_cols)
            fresh = (lax.rem(across, mesh_cols) == column) & (tile != old) & (tile != seen)

            @pl.when(fresh)
            def _():
                link[s * CAP + count] = head[tile]
                head[tile] = s * CAP + count

            return (
                jnp.where(fresh, count + 1, count),
                jnp.where(fresh, seen, old),
                jnp.where(fresh, tile, seen),
            )

        lax.fori_loop(0, kids, child, (jnp.int32(0), jnp.int32(-1), jnp.int32(-1)))
        return carry

    lax.fori_loop(0, mesh_cols, source, 0)

    def walk(tile, n):
        def one(state):
            n, slot = state
            out_ref[n] = tile
            out_ref[total + n] = slot
            return n + 1, link[slot]

        return lax.while_loop(lambda state: state[1] >= 0, one, (n, head[tile]))[0]

    count = lax.fori_loop(0, 32, walk, jnp.int32(0))
    out_ref[2 * total] = count

    def fill(n, carry):
        last = jnp.maximum(count - 1, 0)
        none = count == 0
        out_ref[n] = jnp.where(none, 0, out_ref[last])
        out_ref[total + n] = jnp.where(none, 0, out_ref[total + last])
        return carry

    lax.fori_loop(count, total, fill, 0)


def add_table(info, notes, mesh_rows, mesh_cols, kids):
    smem = pl.BlockSpec(memory_space=pltpu.SMEM)
    total = mesh_cols * CAP
    return pl.pallas_call(
        functools.partial(add_table_kernel, mesh_rows, mesh_cols, kids),
        out_shape=jax.ShapeDtypeStruct((2 * total + 1,), I32),
        in_specs=[smem, smem],
        out_specs=smem,
        scratch_shapes=[pltpu.SMEM((32,), I32), pltpu.SMEM((total,), I32)],
        name="add_table",
    )(info, notes)


def add_children(table, base, arrived):
    rows, cols = base.shape
    deep = 8

    def row_spec():
        return pl.BlockSpec((BLK, cols), lambda n, t: (n, 0))

    return pl.pallas_call(
        add_kernel,
        out_shape=jax.ShapeDtypeStruct(base.shape, F32),
        grid_spec=pltpu.PrefetchScalarGridSpec(
            num_scalar_prefetch=1,
            grid=(rows // BLK,),
            in_specs=[row_spec(), pl.BlockSpec(memory_space=pl.ANY)],
            out_specs=row_spec(),
            scratch_shapes=[
                pltpu.VMEM((deep, BLK, BLK), F32),
                pltpu.SemaphoreType.DMA((deep,)),
                pltpu.SMEM((1,), I32),
            ],
        ),
        input_output_aliases={1: 0},
        compiler_params=pltpu.CompilerParams(vmem_limit_bytes=32 << 20),
        cost_estimate=pl.CostEstimate(flops=4_000_000, bytes_accessed=24 << 20, transcendentals=0),
        name="add_children",
    )(table, base, arrived)


def on_device(front_matrix, child_blocks, child_target, child_place, child_live):
    mesh_rows = lax.axis_size("row")
    mesh_cols = lax.axis_size("col")
    row = lax.axis_index("row")
    column = lax.axis_index("col")
    x, core = column // SIDE, row % 2
    slab = front_matrix[:, :BLK]

    table = jnp.stack([row, column]).astype(I32)

    strip = exchange(slab[:BLK].reshape(mesh_cols, -1, BLK), "col")[:LEADS]
    late = after(slab, strip)
    rows = slab.shape[0] // SIDE
    piece = spread_x([late[q * rows : (q + 1) * rows] for q in range(SIDE)], x)
    uc = col_pieces(after(late, piece))
    share, four = lead_share(strip, core)
    raw = lax.all_gather(after(piece, four), "col", axis=0, tiled=False)
    packed = map_children(child_blocks, child_target, child_place, child_live, mesh_cols)

    note = jnp.zeros((8, BLK), F32)
    note = note.at[0, : child_target.size].set(child_target.reshape(-1).astype(F32))
    share, packed, uc = lax.optimization_barrier(
        (jnp.concatenate([share, note], axis=0), packed, uc)
    )
    uc = lax.all_gather(uc, "row", axis=0, tiled=False)
    own = to_all(share, "col")
    packed = after(packed, own)
    arrived = exchange(packed.reshape(mesh_cols, CAP, BLK, BLK), "col")
    arrived = arrived.reshape(mesh_cols * CAP, BLK, BLK)
    other = swap_cores(own)

    factor, high, low = factor_lead(core[None].astype(I32), own, other)
    base = update_front(table, uc, raw, front_matrix, factor, high, low)
    notes = after(own, base)[:, -8, : child_target.size].astype(I32)
    arrivals = add_table(column[None].astype(I32), notes, mesh_rows, mesh_cols, child_target.shape[0])
    return add_children(arrivals, base, arrived)


def solution(mesh):
    return jax.shard_map(
        on_device,
        mesh=mesh,
        in_specs=(
            P("row", "col"),
            P(("row", "col"), None, None),
            P(("row", "col"), None),
            P(("row", "col"), None, None),
            P(("row", "col"), None),
        ),
        out_specs=P("row", "col"),
        check_vma=False,
    )
```

```python
import functools

import jax
import jax.numpy as jnp
from jax import lax
from jax.experimental import pallas as pl
from jax.experimental.pallas import tpu as pltpu
from jax.sharding import PartitionSpec as P

F32 = jnp.float32
BF16 = jnp.bfloat16
I32 = jnp.int32
BLK = 256
LEADS = 4
CAP = 2
SIDE = 4
NB = 128
HIGHEST = lax.Precision.HIGHEST


def dot_nt(left, right, precision=None):
    return lax.dot_general(
        left, right, (((1,), (1,)), ((), ())), precision=precision, preferred_element_type=F32
    )


def dot_nn(left, right, precision=None):
    return lax.dot_general(
        left, right, (((1,), (0,)), ((), ())), precision=precision, preferred_element_type=F32
    )


def split2(value):
    high = value.astype(BF16)
    return high, (value - high.astype(F32)).astype(BF16)


def shift_z(value, dz):
    return lax.ppermute(value, "row", [(r, (r + 2 * dz) % 8) for r in range(8)])


def swap_cores(value):
    return lax.ppermute(value, "row", [(r, r ^ 1) for r in range(8)])


def ring_gather(value, shift):
    return [value, shift(value, 1), shift(value, -1), shift(value, 2)]


def spread_x(parts, x):
    out = jnp.where(x == 0, parts[0], jnp.zeros_like(parts[0]))
    for q in range(1, SIDE):
        out = out + lax.ppermute(parts[q], "col", [(y, q * SIDE + y) for y in range(SIDE)])
    return out


def after(value, *earlier):
    return lax.optimization_barrier((value,) + earlier)[0]


def exchange(value, axis):
    return lax.all_to_all(value, axis, split_axis=0, concat_axis=0, tiled=True)


def to_all(value, axis):
    copies = lax.axis_size(axis)
    return exchange(jnp.broadcast_to(value[None], (copies,) + value.shape), axis)


LOWER = (((0, 0), (1, 0), (2, 0), (3, 0), (1, 1)), ((2, 1), (3, 1), (2, 2), (3, 2), (3, 3)))


def lead_share(strip, core):
    four = to_all(strip, "row")[:LEADS]
    first, second = [jnp.concatenate([four[i, j] for i, j in half], axis=0) for half in LOWER]
    return jnp.where(core == 0, first, second), four


def col_pieces(slab, core):
    blocks = slab.reshape(8, BLK, BLK)
    out = None
    for h in range(2):
        for q in range(2):
            pairs = []
            for r in range(8):
                for j in range(LEADS):
                    pairs.append((r * 16 + j, (2 * j + q) * 16 + r + 8 * h))
            part = jnp.stack([blocks[4 * q + h], blocks[4 * q + 2 + h]])
            part = lax.ppermute(part, ("row", "col"), pairs)
            out = part if out is None else out + part
    other = swap_cores(out)
    return jnp.concatenate(
        [jnp.where(core == 0, out, other), jnp.where(core == 0, other, out)], axis=0
    )


def factor_block(a, u_ref, e_ref):
    n = a.shape[0]
    ri = lax.broadcasted_iota(I32, (n, n), 0)
    ci = lax.broadcasted_iota(I32, (n, n), 1)
    e = jnp.where(ri == ci, F32(1), F32(0))
    base = 0
    for p in range(0, n, 4):
        off = p - base
        m = a.shape[0]
        cols = [jnp.broadcast_to(a[:, p + v : p + v + 1], (m, n)) for v in range(4)]
        s = [[cols[v][off + i : off + i + 1, :] for v in range(4)] for i in range(4)]
        arow = [a[off + i : off + i + 1, :] for i in range(4)]
        erow = [e[off + i : off + i + 1, :] for i in range(4)]
        inverse = []
        for q in range(4):
            r = F32(1) / s[q][q]
            inverse.append(r)
            low = [None] * 4
            for i in range(q + 1, 4):
                low[i] = s[i][q] * r
            for i in range(q + 1, 4):
                for v in range(q + 1, i + 1):
                    s[i][v] = s[i][v] - low[i] * s[v][q]
                arow[i] = arow[i] - low[i] * arow[q]
                erow[i] = erow[i] - low[i] * erow[q]
        for q in range(4):
            scale = lax.rsqrt(s[q][q])
            u_ref[p + q : p + q + 1, :] = arow[q] * scale
            e_ref[p + q : p + q + 1, :] = erow[q] * scale
        following = p + 4
        if following >= n:
            break
        live = None
        if following % 8 == 0:
            cut = following - base
            a, e, cols = a[cut:], e[cut:], [c[cut:] for c in cols]
            base = following
        else:
            live = lax.broadcasted_iota(I32, a.shape, 0) >= following - base
        times = []
        for q in range(4):
            c = cols[q]
            for v in range(q):
                c = c - times[v] * s[q][v]
            times.append(c * inverse[q])
        da = times[0] * arow[0]
        de = times[0] * erow[0]
        for q in range(1, 4):
            da = da + times[q] * arow[q]
            de = de + times[q] * erow[q]
        if live is not None:
            da = jnp.where(live, da, F32(0))
            de = jnp.where(live, de, F32(0))
        a = a - da
        e = e - de


def factor_kernel(table, own_ref, other_ref, l_ref, high_ref, low_ref, m_ref, inv_ref, u_ref, e_ref):
    n = m_ref.shape[0]
    steps = n // NB
    strips = own_ref.shape[0]
    tall = BLK // strips

    def assemble(sources):
        def place(number, carry):
            for half, source in zip(LOWER, sources):
                for spot, (i, j) in enumerate(half):
                    row = pl.multiple_of(i * BLK + number * tall, tall)
                    m_ref[pl.ds(row, tall), j * BLK : (j + 1) * BLK] = source[
                        number, spot * tall : (spot + 1) * tall, :
                    ]
            return carry

        lax.fori_loop(0, strips, place, 0)

    @pl.when(table[0] == 0)
    def _():
        assemble((own_ref, other_ref))

    @pl.when(table[0] != 0)
    def _():
        assemble((other_ref, own_ref))

    l_ref[...] = jnp.zeros_like(l_ref)
    inv_ref[...] = jnp.zeros_like(inv_ref)
    ri = lax.broadcasted_iota(I32, (NB, NB), 0)
    ci = lax.broadcasted_iota(I32, (NB, NB), 1)

    def step(k, carry):
        at = pl.multiple_of(k * NB, NB)
        d = m_ref[pl.ds(at, NB), pl.ds(at, NB)]
        factor_block(jnp.where(ri >= ci, d, d.T), u_ref, e_ref)
        l_ref[pl.ds(at, NB), pl.ds(at, NB)] = jnp.where(ri <= ci, u_ref[...], F32(0)).T
        ik = jnp.where(ri >= ci, e_ref[...], F32(0))
        for kk in range(steps):

            @pl.when(k == kk)
            def _():
                lo, hi = kk * NB, (kk + 1) * NB
                if kk < steps - 1:
                    panel = dot_nt(m_ref[hi:, lo:hi], ik, HIGHEST)
                    l_ref[hi:, lo:hi] = panel
                    m_ref[hi:, hi:] = m_ref[hi:, hi:] - dot_nt(panel, panel, HIGHEST)
                if kk > 0:
                    inv_ref[lo:hi, :lo] = dot_nn(ik, inv_ref[lo:hi, :lo], HIGHEST)
                inv_ref[lo:hi, lo:hi] = ik
                if kk < steps - 1:
                    inv_ref[hi:, :hi] = inv_ref[hi:, :hi] - dot_nn(
                        panel, inv_ref[lo:hi, :hi], HIGHEST
                    )

        return carry

    lax.fori_loop(0, steps, step, 0)
    for i in range(LEADS):
        rows = slice(i * BLK, (i + 1) * BLK)
        high_ref[rows, :], low_ref[rows, :] = split2(inv_ref[rows, :])


def factor_lead(table, *parts):
    n = LEADS * BLK
    vmem = pl.BlockSpec(memory_space=pltpu.VMEM)
    return pl.pallas_call(
        factor_kernel,
        out_shape=(
            jax.ShapeDtypeStruct((n, n), F32),
            jax.ShapeDtypeStruct((n, n), BF16),
            jax.ShapeDtypeStruct((n, n), BF16),
        ),
        in_specs=[pl.BlockSpec(memory_space=pltpu.SMEM)] + [vmem] * 2,
        out_specs=[vmem, vmem, vmem],
        scratch_shapes=[
            pltpu.VMEM((n, n), F32),
            pltpu.VMEM((n, n), F32),
            pltpu.VMEM((NB, NB), F32),
            pltpu.VMEM((NB, NB), F32),
        ],
        compiler_params=pltpu.CompilerParams(vmem_limit_bytes=40 << 20),
        cost_estimate=pl.CostEstimate(flops=60_000_000_000, bytes_accessed=10 << 20, transcendentals=0),
        name="factor_lead",
    )(table, *parts)


def update_kernel(table, *refs):
    uc, raw = refs[0:4], refs[4:8]
    front_ref, own_ref, high_ref, low_ref, out_ref = refs[8:13]
    ch, cl, rh, rl, pan = refs[13:]
    g = pl.program_id(0)
    r, c = table[4], table[5]

    def put(rows, spot, value):
        cols = pl.ds(pl.multiple_of(spot * BLK, BLK), BLK)
        rh[rows, cols], rl[rows, cols] = split2(value)

    upper, lower = slice(0, BLK), slice(BLK, 2 * BLK)

    def solve():
        high, low = rh[...], rl[...]
        out = []
        for j in range(LEADS):
            hi = (j + 1) * BLK
            rows = slice(j * BLK, hi)
            out.append(
                dot_nt(high[:, :hi], high_ref[rows, :hi])
                + (
                    dot_nt(high[:, :hi], low_ref[rows, :hi])
                    + dot_nt(low[:, :hi], high_ref[rows, :hi])
                )
            )
        return out

    @pl.when(g < 2)
    def _():
        for q in range(SIDE):
            put(upper, table[q], uc[q][0])
            put(lower, table[q], uc[q][1])
        got = solve()
        at = pl.ds(pl.multiple_of(g * 2 * BLK, BLK), 2 * BLK)
        for j in range(LEADS):
            cols = slice(j * BLK, (j + 1) * BLK)
            ch[at, cols], cl[at, cols] = split2(got[j])

    @pl.when(g >= 2)
    def _():
        for j in range(LEADS):
            cols = slice(j * BLK, (j + 1) * BLK)
            rh[:, cols], rl[:, cols] = split2(raw[j][0])
        got = solve()
        special = (g == 2) & (r < LEADS)
        top = lax.broadcasted_iota(I32, (2 * BLK, BLK), 0) < BLK
        left = []
        for j in range(LEADS):
            cols = slice(j * BLK, (j + 1) * BLK)
            own = own_ref[:, cols]
            own = jnp.concatenate([own, own], axis=0)
            keep = jnp.where((r >= 2) & (j < 2), F32(1), F32(0))
            left.append(jnp.where(top & special, own * keep, got[j]))

            @pl.when(c == j)
            def _():
                pan[...] = jnp.where(top & special, own, got[j])

        left_h, left_l = split2(jnp.concatenate(left, axis=1))
        for t in range(4):
            rows = slice(t * BLK, (t + 1) * BLK)
            right_h, right_l = ch[rows, :], cl[rows, :]
            out_ref[:, rows] = front_ref[:, rows] - (
                dot_nt(left_h, right_h) + (dot_nt(left_h, right_l) + dot_nt(left_l, right_h))
            )

        @pl.when(c < LEADS)
        def _():
            out_ref[:, :BLK] = pan[...]


def update_front(table, uc, raw, front, factor, high, low):
    n = LEADS * BLK
    rows, cols = front.shape
    tall = 2 * BLK

    def step(g):
        return jnp.maximum(g - 2, 0)

    def tall_spec():
        return pl.BlockSpec((tall, cols), lambda g, t: (step(g), 0))

    def raw_spec(j):
        return pl.BlockSpec((1, tall, BLK), lambda g, t: (step(g) * SIDE + j, 0, 0))

    in_specs = [pl.BlockSpec((2, BLK, BLK), lambda g, t: (jnp.minimum(g, 1), 0, 0))] * SIDE
    in_specs += [raw_spec(j) for j in range(LEADS)]
    in_specs += [
        tall_spec(),
        pl.BlockSpec((BLK, n), lambda g, t: (jnp.minimum(t[4], LEADS - 1), 0)),
        pl.BlockSpec((n, n), lambda g, t: (0, 0)),
        pl.BlockSpec((n, n), lambda g, t: (0, 0)),
    ]
    return pl.pallas_call(
        update_kernel,
        out_shape=jax.ShapeDtypeStruct((rows, cols), F32),
        grid_spec=pltpu.PrefetchScalarGridSpec(
            num_scalar_prefetch=1,
            grid=(2 + rows // tall,),
            in_specs=in_specs,
            out_specs=tall_spec(),
            scratch_shapes=[
                pltpu.VMEM((n, n), BF16),
                pltpu.VMEM((n, n), BF16),
                pltpu.VMEM((tall, n), BF16),
                pltpu.VMEM((tall, n), BF16),
                pltpu.VMEM((tall, BLK), F32),
            ],
        ),
        compiler_params=pltpu.CompilerParams(vmem_limit_bytes=58 << 20),
        cost_estimate=pl.CostEstimate(flops=26_000_000_000, bytes_accessed=36 << 20, transcendentals=0),
        name="update_front",
    )(table, *uc, *([raw] * LEADS), front, factor, high, low)


def slots_of(target, mesh_cols):
    kids = target.shape[-2]
    same = jnp.all(target[..., :, None, :] == target[..., None, :, :], axis=-1)
    number = jnp.arange(kids, dtype=I32)
    first = jnp.min(jnp.where(same, number, kids), axis=-1)
    leads = first == number
    goal = target[..., 1] % mesh_cols
    alike = (goal[..., :, None] == goal[..., None, :]) & leads[..., None, :]
    rank = jnp.sum((alike & (number < first[..., :, None])).astype(I32), axis=-1)
    return rank * mesh_cols + goal, leads


def sort_order(keys):
    count = keys.shape[0]
    number = jnp.arange(count, dtype=I32)
    before = (keys[None, :] < keys[:, None]) | (
        (keys[None, :] == keys[:, None]) & (number[None, :] < number[:, None])
    )
    place = jnp.sum(before.astype(I32), axis=1)
    hot = (place[None, :] == number[:, None]).astype(I32)
    return lambda values: jnp.sum(hot * values[None, :], axis=1)


def map_kernel(table, block_ref, place_ref, out_ref):
    k = pl.program_id(0)
    live_row, live_col = table[16 + k], table[24 + k]
    target = lax.broadcasted_iota(I32, (BLK, BLK), 0)
    source = lax.broadcasted_iota(I32, (BLK, BLK), 1)

    def picks(index, live):
        hit = (place_ref[0, index : index + 1, :] == target) & (source < live)
        return jnp.where(hit, F32(1), F32(0)).astype(BF16)

    def parts(value):
        high = value.astype(BF16)
        rest = value - high.astype(F32)
        middle = rest.astype(BF16)
        return high, middle, (rest - middle.astype(F32)).astype(BF16)

    row_pick, col_pick = picks(0, live_row), picks(1, live_col)
    high, middle, low = parts(block_ref[0])
    moved = dot_nn(row_pick, high) + (dot_nn(row_pick, middle) + dot_nn(row_pick, low))
    high, middle, low = parts(moved)
    mapped = dot_nt(high, col_pick) + (dot_nt(middle, col_pick) + dot_nt(low, col_pick))
    opens = (k == 0) | (table[8 + k] != table[8 + jnp.maximum(k - 1, 0)])

    @pl.when(opens)
    def _():
        out_ref[0] = mapped

    @pl.when(jnp.logical_not(opens))
    def _():
        out_ref[0] = out_ref[0] + mapped


def map_children(child_blocks, child_target, child_place, child_live, mesh_cols):
    kids = child_blocks.shape[0]
    slot, _ = slots_of(child_target, mesh_cols)
    ordered = sort_order(slot)
    table = jnp.concatenate(
        [
            ordered(jnp.arange(kids, dtype=I32)),
            ordered(slot),
            ordered(child_live[:, 0]),
            ordered(child_live[:, 1]),
        ]
    )
    return pl.pallas_call(
        map_kernel,
        out_shape=jax.ShapeDtypeStruct((mesh_cols * CAP, BLK, BLK), F32),
        grid_spec=pltpu.PrefetchScalarGridSpec(
            num_scalar_prefetch=1,
            grid=(kids,),
            in_specs=[
                pl.BlockSpec((1, BLK, BLK), lambda k, t: (t[k], 0, 0)),
                pl.BlockSpec((1, 2, BLK), lambda k, t: (t[k], 0, 0)),
            ],
            out_specs=pl.BlockSpec((1, BLK, BLK), lambda k, t: (t[8 + k], 0, 0)),
        ),
        cost_estimate=pl.CostEstimate(flops=2_000_000_000, bytes_accessed=4 << 20, transcendentals=0),
        name="map_children",
    )(table, child_blocks, child_place)


def add_kernel(table, base_ref, first_ref, second_ref, out_ref, buffers, sems, next_ref):
    row = pl.program_id(0)
    total = 32
    count = table[2 * total]
    deep = buffers.shape[0]
    parts = (first_ref, second_ref)
    each = total // len(parts)

    def copy(n, part, at):
        k = lax.rem(n, deep)
        return pltpu.make_async_copy(part.at[at], buffers.at[k], sems.at[k])

    def start(n):
        slot = table[total + n]
        for q, part in enumerate(parts):

            @pl.when(lax.div(slot, each) == q)
            def _():
                copy(n, part, slot - q * each).start()

    @pl.when(row == 0)
    def _():
        next_ref[0] = 0
        for n in range(deep):

            @pl.when(n < count)
            def _():
                start(jnp.int32(n))

    out_ref[...] = base_ref[...]

    def here(n):
        return (n < count) & (lax.div(table[jnp.minimum(n, total - 1)], 4) == row)

    def add(n):
        copy(n, first_ref, 0).wait()
        cols = pl.ds(pl.multiple_of(lax.rem(table[n], 4) * BLK, BLK), BLK)
        out_ref[:, cols] = out_ref[:, cols] + buffers[lax.rem(n, deep)]

        @pl.when(n + deep < count)
        def _():
            start(n + deep)

        return n + 1

    next_ref[0] = lax.while_loop(here, add, next_ref[0])


def add_table_kernel(mesh_rows, mesh_cols, kids, info_ref, notes_ref, out_ref, head, link):
    total = mesh_cols * CAP
    column = info_ref[0]

    def clear(n, carry):
        head[n] = -1
        return carry

    lax.fori_loop(0, 32, clear, 0)

    def source(s, carry):

        def child(k, found):
            count, old, seen = found
            down, across = notes_ref[s, 2 * k], notes_ref[s, 2 * k + 1]
            tile = lax.div(down, mesh_rows) * 4 + lax.div(across, mesh_cols)
            fresh = (lax.rem(across, mesh_cols) == column) & (tile != old) & (tile != seen)

            @pl.when(fresh)
            def _():
                link[count * mesh_cols + s] = head[tile]
                head[tile] = count * mesh_cols + s

            return (
                jnp.where(fresh, count + 1, count),
                jnp.where(fresh, seen, old),
                jnp.where(fresh, tile, seen),
            )

        lax.fori_loop(0, kids, child, (jnp.int32(0), jnp.int32(-1), jnp.int32(-1)))
        return carry

    lax.fori_loop(0, mesh_cols, source, 0)

    def walk(tile, n):
        def one(state):
            n, slot = state
            out_ref[n] = tile
            out_ref[total + n] = slot
            return n + 1, link[slot]

        return lax.while_loop(lambda state: state[1] >= 0, one, (n, head[tile]))[0]

    count = lax.fori_loop(0, 32, walk, jnp.int32(0))
    out_ref[2 * total] = count

    def fill(n, carry):
        last = jnp.maximum(count - 1, 0)
        none = count == 0
        out_ref[n] = jnp.where(none, 0, out_ref[last])
        out_ref[total + n] = jnp.where(none, 0, out_ref[total + last])
        return carry

    lax.fori_loop(count, total, fill, 0)


def add_table(info, notes, mesh_rows, mesh_cols, kids):
    smem = pl.BlockSpec(memory_space=pltpu.SMEM)
    total = mesh_cols * CAP
    return pl.pallas_call(
        functools.partial(add_table_kernel, mesh_rows, mesh_cols, kids),
        out_shape=jax.ShapeDtypeStruct((2 * total + 1,), I32),
        in_specs=[smem, smem],
        out_specs=smem,
        scratch_shapes=[pltpu.SMEM((32,), I32), pltpu.SMEM((total,), I32)],
        name="add_table",
    )(info, notes)


def add_children(table, base, first, second):
    rows, cols = base.shape
    deep = 8

    def row_spec():
        return pl.BlockSpec((BLK, cols), lambda n, t: (n, 0))

    return pl.pallas_call(
        add_kernel,
        out_shape=jax.ShapeDtypeStruct(base.shape, F32),
        grid_spec=pltpu.PrefetchScalarGridSpec(
            num_scalar_prefetch=1,
            grid=(rows // BLK,),
            in_specs=[row_spec()] + [pl.BlockSpec(memory_space=pl.ANY)] * 2,
            out_specs=row_spec(),
            scratch_shapes=[
                pltpu.VMEM((deep, BLK, BLK), F32),
                pltpu.SemaphoreType.DMA((deep,)),
                pltpu.SMEM((1,), I32),
            ],
        ),
        input_output_aliases={1: 0},
        compiler_params=pltpu.CompilerParams(vmem_limit_bytes=32 << 20),
        cost_estimate=pl.CostEstimate(flops=4_000_000, bytes_accessed=24 << 20, transcendentals=0),
        name="add_children",
    )(table, base, first, second)


def on_device(front_matrix, child_blocks, child_target, child_place, child_live):
    mesh_rows = lax.axis_size("row")
    mesh_cols = lax.axis_size("col")
    row = lax.axis_index("row")
    column = lax.axis_index("col")
    x, y, z, core = column // SIDE, column % SIDE, row // 2, row % 2
    slab = front_matrix[:, :BLK]

    offset = jnp.array([0, -1, 1, 2], I32)
    table = jnp.concatenate([(z + offset) % SIDE, row[None], column[None]]).astype(I32)

    strip = exchange(slab[:BLK].reshape(mesh_cols, -1, BLK), "col")[:LEADS]
    late = after(slab, strip)
    rows = slab.shape[0] // SIDE
    piece = spread_x([late[q * rows : (q + 1) * rows] for q in range(SIDE)], x)
    uc = col_pieces(late, core)
    share, four = lead_share(strip, core)
    raw = lax.all_gather(after(piece, four), "col", axis=0, tiled=False)
    packed = map_children(child_blocks, child_target, child_place, child_live, mesh_cols)

    note = jnp.zeros((8, BLK), F32)
    note = note.at[0, : child_target.size].set(child_target.reshape(-1).astype(F32))
    share = after(jnp.concatenate([share, note], axis=0), packed)
    uc = ring_gather(after(uc, four), shift_z)
    own = to_all(share, "col")
    first, second = packed[:mesh_cols], packed[mesh_cols:]
    first = exchange(after(first, own), "col")
    other = swap_cores(own)

    factor, high, low = factor_lead(core[None].astype(I32), own, other)
    notes = after(own, factor)[:, -8, : child_target.size].astype(I32)
    arrivals = add_table(column[None].astype(I32), notes, mesh_rows, mesh_cols, child_target.shape[0])
    second = exchange(after(second, factor), "col")
    base = update_front(table, uc, raw, front_matrix, factor, high, low)
    return add_children(arrivals, base, first, second)


def solution(mesh):
    return jax.shard_map(
        on_device,
        mesh=mesh,
        in_specs=(
            P("row", "col"),
            P(("row", "col"), None, None),
            P(("row", "col"), None),
            P(("row", "col"), None, None),
            P(("row", "col"), None),
        ),
        out_specs=P("row", "col"),
        check_vma=False,
    )
```

```python
import functools

import jax
import jax.numpy as jnp
from jax import lax
from jax.experimental import pallas as pl
from jax.experimental.pallas import tpu as pltpu
from jax.sharding import PartitionSpec as P

F32 = jnp.float32
BF16 = jnp.bfloat16
I32 = jnp.int32
BLK = 256
LEADS = 4
CAP = 2
SIDE = 4
NB = 128
HIGHEST = lax.Precision.HIGHEST


def dot_nt(left, right, precision=None):
    return lax.dot_general(
        left, right, (((1,), (1,)), ((), ())), precision=precision, preferred_element_type=F32
    )


def dot_nn(left, right, precision=None):
    return lax.dot_general(
        left, right, (((1,), (0,)), ((), ())), precision=precision, preferred_element_type=F32
    )


def split2(value):
    high = value.astype(BF16)
    return high, (value - high.astype(F32)).astype(BF16)


def shift_z(value, dz):
    return lax.ppermute(value, "row", [(r, (r + 2 * dz) % 8) for r in range(8)])


def swap_cores(value):
    return lax.ppermute(value, "row", [(r, r ^ 1) for r in range(8)])


def ring_gather(value, shift):
    return [value, shift(value, 1), shift(value, -1), shift(value, 2)]


def spread_x(parts, x):
    out = jnp.where(x == 0, parts[0], jnp.zeros_like(parts[0]))
    for q in range(1, SIDE):
        out = out + lax.ppermute(parts[q], "col", [(y, q * SIDE + y) for y in range(SIDE)])
    return out


def after(value, *earlier):
    return lax.optimization_barrier((value,) + earlier)[0]


def exchange(value, axis):
    return lax.all_to_all(value, axis, split_axis=0, concat_axis=0, tiled=True)


def to_all(value, axis):
    copies = lax.axis_size(axis)
    return exchange(jnp.broadcast_to(value[None], (copies,) + value.shape), axis)


LOWER = (((0, 0), (1, 0), (2, 0), (3, 0), (1, 1)), ((2, 1), (3, 1), (2, 2), (3, 2), (3, 3)))


def lead_share(strip, core):
    four = to_all(strip, "row")[:LEADS]
    first, second = [jnp.concatenate([four[i, j] for i, j in half], axis=0) for half in LOWER]
    return jnp.where(core == 0, first, second), four


def col_pieces(slab, core):
    blocks = slab.reshape(8, BLK, BLK)
    out = None
    for h in range(2):
        for q in range(2):
            pairs = []
            for r in range(8):
                for j in range(LEADS):
                    pairs.append((r * 16 + j, (2 * j + q) * 16 + r + 8 * h))
            part = jnp.stack([blocks[4 * q + h], blocks[4 * q + 2 + h]])
            part = lax.ppermute(part, ("row", "col"), pairs)
            out = part if out is None else out + part
    other = swap_cores(out)
    return jnp.concatenate(
        [jnp.where(core == 0, out, other), jnp.where(core == 0, other, out)], axis=0
    )


def factor_block(a, u_ref, e_ref):
    n = a.shape[0]
    ri = lax.broadcasted_iota(I32, (n, n), 0)
    ci = lax.broadcasted_iota(I32, (n, n), 1)
    e = jnp.where(ri == ci, F32(1), F32(0))
    base = 0
    for p in range(0, n, 4):
        off = p - base
        m = a.shape[0]
        cols = [jnp.broadcast_to(a[:, p + v : p + v + 1], (m, n)) for v in range(4)]
        s = [[cols[v][off + i : off + i + 1, :] for v in range(4)] for i in range(4)]
        arow = [a[off + i : off + i + 1, :] for i in range(4)]
        erow = [e[off + i : off + i + 1, :] for i in range(4)]
        inverse = []
        for q in range(4):
            r = F32(1) / s[q][q]
            inverse.append(r)
            low = [None] * 4
            for i in range(q + 1, 4):
                low[i] = s[i][q] * r
            for i in range(q + 1, 4):
                for v in range(q + 1, i + 1):
                    s[i][v] = s[i][v] - low[i] * s[v][q]
                arow[i] = arow[i] - low[i] * arow[q]
                erow[i] = erow[i] - low[i] * erow[q]
        for q in range(4):
            scale = lax.rsqrt(s[q][q])
            u_ref[p + q : p + q + 1, :] = arow[q] * scale
            e_ref[p + q : p + q + 1, :] = erow[q] * scale
        following = p + 4
        if following >= n:
            break
        live = None
        if following % 8 == 0:
            cut = following - base
            a, e, cols = a[cut:], e[cut:], [c[cut:] for c in cols]
            base = following
        else:
            live = lax.broadcasted_iota(I32, a.shape, 0) >= following - base
        times = []
        for q in range(4):
            c = cols[q]
            for v in range(q):
                c = c - times[v] * s[q][v]
            times.append(c * inverse[q])
        da = times[0] * arow[0]
        de = times[0] * erow[0]
        for q in range(1, 4):
            da = da + times[q] * arow[q]
            de = de + times[q] * erow[q]
        if live is not None:
            da = jnp.where(live, da, F32(0))
            de = jnp.where(live, de, F32(0))
        a = a - da
        e = e - de


def factor_kernel(table, own_ref, other_ref, l_ref, high_ref, low_ref, m_ref, inv_ref, u_ref, e_ref):
    n = m_ref.shape[0]
    steps = n // NB
    strips = own_ref.shape[0]
    tall = BLK // strips

    def assemble(sources):
        def place(number, carry):
            for half, source in zip(LOWER, sources):
                for spot, (i, j) in enumerate(half):
                    row = pl.multiple_of(i * BLK + number * tall, tall)
                    m_ref[pl.ds(row, tall), j * BLK : (j + 1) * BLK] = source[
                        number, spot * tall : (spot + 1) * tall, :
                    ]
            return carry

        lax.fori_loop(0, strips, place, 0)

    @pl.when(table[0] == 0)
    def _():
        assemble((own_ref, other_ref))

    @pl.when(table[0] != 0)
    def _():
        assemble((other_ref, own_ref))

    l_ref[...] = jnp.zeros_like(l_ref)
    inv_ref[...] = jnp.zeros_like(inv_ref)
    ri = lax.broadcasted_iota(I32, (NB, NB), 0)
    ci = lax.broadcasted_iota(I32, (NB, NB), 1)

    def step(k, carry):
        at = pl.multiple_of(k * NB, NB)
        d = m_ref[pl.ds(at, NB), pl.ds(at, NB)]
        factor_block(jnp.where(ri >= ci, d, d.T), u_ref, e_ref)
        l_ref[pl.ds(at, NB), pl.ds(at, NB)] = jnp.where(ri <= ci, u_ref[...], F32(0)).T
        ik = jnp.where(ri >= ci, e_ref[...], F32(0))
        for kk in range(steps):

            @pl.when(k == kk)
            def _():
                lo, hi = kk * NB, (kk + 1) * NB
                if kk < steps - 1:
                    panel = dot_nt(m_ref[hi:, lo:hi], ik, HIGHEST)
                    l_ref[hi:, lo:hi] = panel
                    m_ref[hi:, hi:] = m_ref[hi:, hi:] - dot_nt(panel, panel, HIGHEST)
                if kk > 0:
                    inv_ref[lo:hi, :lo] = dot_nn(ik, inv_ref[lo:hi, :lo], HIGHEST)
                inv_ref[lo:hi, lo:hi] = ik
                if kk < steps - 1:
                    inv_ref[hi:, :hi] = inv_ref[hi:, :hi] - dot_nn(
                        panel, inv_ref[lo:hi, :hi], HIGHEST
                    )

        return carry

    lax.fori_loop(0, steps, step, 0)
    for i in range(LEADS):
        rows = slice(i * BLK, (i + 1) * BLK)
        high_ref[rows, :], low_ref[rows, :] = split2(inv_ref[rows, :])


def factor_lead(table, *parts):
    n = LEADS * BLK
    vmem = pl.BlockSpec(memory_space=pltpu.VMEM)
    return pl.pallas_call(
        factor_kernel,
        out_shape=(
            jax.ShapeDtypeStruct((n, n), F32),
            jax.ShapeDtypeStruct((n, n), BF16),
            jax.ShapeDtypeStruct((n, n), BF16),
        ),
        in_specs=[pl.BlockSpec(memory_space=pltpu.SMEM)] + [vmem] * 2,
        out_specs=[vmem, vmem, vmem],
        scratch_shapes=[
            pltpu.VMEM((n, n), F32),
            pltpu.VMEM((n, n), F32),
            pltpu.VMEM((NB, NB), F32),
            pltpu.VMEM((NB, NB), F32),
        ],
        compiler_params=pltpu.CompilerParams(vmem_limit_bytes=40 << 20),
        cost_estimate=pl.CostEstimate(flops=60_000_000_000, bytes_accessed=10 << 20, transcendentals=0),
        name="factor_lead",
    )(table, *parts)


def update_kernel(table, *refs):
    uc, raw = refs[0:4], refs[4:8]
    front_ref, own_ref, high_ref, low_ref, out_ref = refs[8:13]
    ch, cl, rh, rl, pan = refs[13:]
    g = pl.program_id(0)
    r, c = table[4], table[5]

    def put(rows, spot, value):
        cols = pl.ds(pl.multiple_of(spot * BLK, BLK), BLK)
        rh[rows, cols], rl[rows, cols] = split2(value)

    upper, lower = slice(0, BLK), slice(BLK, 2 * BLK)

    def solve():
        high, low = rh[...], rl[...]
        out = []
        for j in range(LEADS):
            hi = (j + 1) * BLK
            rows = slice(j * BLK, hi)
            out.append(
                dot_nt(high[:, :hi], high_ref[rows, :hi])
                + (
                    dot_nt(high[:, :hi], low_ref[rows, :hi])
                    + dot_nt(low[:, :hi], high_ref[rows, :hi])
                )
            )
        return out

    @pl.when(g < 2)
    def _():
        for q in range(SIDE):
            put(upper, table[q], uc[q][0])
            put(lower, table[q], uc[q][1])
        got = solve()
        at = pl.ds(pl.multiple_of(g * 2 * BLK, BLK), 2 * BLK)
        for j in range(LEADS):
            cols = slice(j * BLK, (j + 1) * BLK)
            ch[at, cols], cl[at, cols] = split2(got[j])

    @pl.when(g >= 2)
    def _():
        for j in range(LEADS):
            cols = slice(j * BLK, (j + 1) * BLK)
            rh[:, cols], rl[:, cols] = split2(raw[j][0])
        got = solve()
        special = (g == 2) & (r < LEADS)
        top = lax.broadcasted_iota(I32, (2 * BLK, BLK), 0) < BLK
        left = []
        for j in range(LEADS):
            cols = slice(j * BLK, (j + 1) * BLK)
            own = own_ref[:, cols]
            own = jnp.concatenate([own, own], axis=0)
            keep = jnp.where((r >= 2) & (j < 2), F32(1), F32(0))
            left.append(jnp.where(top & special, own * keep, got[j]))

            @pl.when(c == j)
            def _():
                pan[...] = jnp.where(top & special, own, got[j])

        left_h, left_l = split2(jnp.concatenate(left, axis=1))
        for t in range(4):
            rows = slice(t * BLK, (t + 1) * BLK)
            right_h, right_l = ch[rows, :], cl[rows, :]
            out_ref[:, rows] = front_ref[:, rows] - (
                dot_nt(left_h, right_h) + (dot_nt(left_h, right_l) + dot_nt(left_l, right_h))
            )

        @pl.when(c < LEADS)
        def _():
            out_ref[:, :BLK] = pan[...]


def update_front(table, uc, raw, front, factor, high, low):
    n = LEADS * BLK
    rows, cols = front.shape
    tall = 2 * BLK

    def step(g):
        return jnp.maximum(g - 2, 0)

    def tall_spec():
        return pl.BlockSpec((tall, cols), lambda g, t: (step(g), 0))

    def raw_spec(j):
        return pl.BlockSpec((1, tall, BLK), lambda g, t: (step(g) * SIDE + j, 0, 0))

    in_specs = [pl.BlockSpec((2, BLK, BLK), lambda g, t: (jnp.minimum(g, 1), 0, 0))] * SIDE
    in_specs += [raw_spec(j) for j in range(LEADS)]
    in_specs += [
        tall_spec(),
        pl.BlockSpec((BLK, n), lambda g, t: (jnp.minimum(t[4], LEADS - 1), 0)),
        pl.BlockSpec((n, n), lambda g, t: (0, 0)),
        pl.BlockSpec((n, n), lambda g, t: (0, 0)),
    ]
    return pl.pallas_call(
        update_kernel,
        out_shape=jax.ShapeDtypeStruct((rows, cols), F32),
        grid_spec=pltpu.PrefetchScalarGridSpec(
            num_scalar_prefetch=1,
            grid=(2 + rows // tall,),
            in_specs=in_specs,
            out_specs=tall_spec(),
            scratch_shapes=[
                pltpu.VMEM((n, n), BF16),
                pltpu.VMEM((n, n), BF16),
                pltpu.VMEM((tall, n), BF16),
                pltpu.VMEM((tall, n), BF16),
                pltpu.VMEM((tall, BLK), F32),
            ],
        ),
        compiler_params=pltpu.CompilerParams(vmem_limit_bytes=58 << 20),
        cost_estimate=pl.CostEstimate(flops=26_000_000_000, bytes_accessed=36 << 20, transcendentals=0),
        name="update_front",
    )(table, *uc, *([raw] * LEADS), front, factor, high, low)


def slots_of(target, mesh_cols):
    kids = target.shape[-2]
    same = jnp.all(target[..., :, None, :] == target[..., None, :, :], axis=-1)
    number = jnp.arange(kids, dtype=I32)
    first = jnp.min(jnp.where(same, number, kids), axis=-1)
    leads = first == number
    goal = target[..., 1] % mesh_cols
    alike = (goal[..., :, None] == goal[..., None, :]) & leads[..., None, :]
    rank = jnp.sum((alike & (number < first[..., :, None])).astype(I32), axis=-1)
    return rank * mesh_cols + goal, leads


def sort_order(keys):
    count = keys.shape[0]
    number = jnp.arange(count, dtype=I32)
    before = (keys[None, :] < keys[:, None]) | (
        (keys[None, :] == keys[:, None]) & (number[None, :] < number[:, None])
    )
    place = jnp.sum(before.astype(I32), axis=1)
    hot = (place[None, :] == number[:, None]).astype(I32)
    return lambda values: jnp.sum(hot * values[None, :], axis=1)


def map_kernel(table, block_ref, place_ref, out_ref):
    k = pl.program_id(0)
    live_row, live_col = table[16 + k], table[24 + k]
    target = lax.broadcasted_iota(I32, (BLK, BLK), 0)
    source = lax.broadcasted_iota(I32, (BLK, BLK), 1)

    def picks(index, live):
        hit = (place_ref[0, index : index + 1, :] == target) & (source < live)
        return jnp.where(hit, F32(1), F32(0)).astype(BF16)

    def parts(value):
        high = value.astype(BF16)
        rest = value - high.astype(F32)
        middle = rest.astype(BF16)
        return high, middle, (rest - middle.astype(F32)).astype(BF16)

    row_pick, col_pick = picks(0, live_row), picks(1, live_col)
    high, middle, low = parts(block_ref[0])
    moved = dot_nn(row_pick, high) + (dot_nn(row_pick, middle) + dot_nn(row_pick, low))
    high, middle, low = parts(moved)
    mapped = dot_nt(high, col_pick) + (dot_nt(middle, col_pick) + dot_nt(low, col_pick))
    opens = (k == 0) | (table[8 + k] != table[8 + jnp.maximum(k - 1, 0)])

    @pl.when(opens)
    def _():
        out_ref[0] = mapped

    @pl.when(jnp.logical_not(opens))
    def _():
        out_ref[0] = out_ref[0] + mapped


def map_children(child_blocks, child_target, child_place, child_live, mesh_cols):
    kids = child_blocks.shape[0]
    slot, _ = slots_of(child_target, mesh_cols)
    ordered = sort_order(slot)
    table = jnp.concatenate(
        [
            ordered(jnp.arange(kids, dtype=I32)),
            ordered(slot),
            ordered(child_live[:, 0]),
            ordered(child_live[:, 1]),
        ]
    )
    return pl.pallas_call(
        map_kernel,
        out_shape=jax.ShapeDtypeStruct((mesh_cols * CAP, BLK, BLK), F32),
        grid_spec=pltpu.PrefetchScalarGridSpec(
            num_scalar_prefetch=1,
            grid=(kids,),
            in_specs=[
                pl.BlockSpec((1, BLK, BLK), lambda k, t: (t[k], 0, 0)),
                pl.BlockSpec((1, 2, BLK), lambda k, t: (t[k], 0, 0)),
            ],
            out_specs=pl.BlockSpec((1, BLK, BLK), lambda k, t: (t[8 + k], 0, 0)),
        ),
        cost_estimate=pl.CostEstimate(flops=2_000_000_000, bytes_accessed=4 << 20, transcendentals=0),
        name="map_children",
    )(table, child_blocks, child_place)


def add_kernel(table, base_ref, first_ref, second_ref, out_ref, buffers, sems, next_ref):
    row = pl.program_id(0)
    total = 32
    count = table[2 * total]
    deep = buffers.shape[0]
    parts = (first_ref, second_ref)
    each = total // len(parts)

    def copy(n, part, at):
        k = lax.rem(n, deep)
        return pltpu.make_async_copy(part.at[at], buffers.at[k], sems.at[k])

    def start(n):
        slot = table[total + n]
        for q, part in enumerate(parts):

            @pl.when(lax.div(slot, each) == q)
            def _():
                copy(n, part, slot - q * each).start()

    @pl.when(row == 0)
    def _():
        next_ref[0] = 0
        for n in range(deep):

            @pl.when(n < count)
            def _():
                start(jnp.int32(n))

    out_ref[...] = base_ref[...]

    def here(n):
        return (n < count) & (lax.div(table[jnp.minimum(n, total - 1)], 4) == row)

    def add(n):
        copy(n, first_ref, 0).wait()
        cols = pl.ds(pl.multiple_of(lax.rem(table[n], 4) * BLK, BLK), BLK)
        out_ref[:, cols] = out_ref[:, cols] + buffers[lax.rem(n, deep)]

        @pl.when(n + deep < count)
        def _():
            start(n + deep)

        return n + 1

    next_ref[0] = lax.while_loop(here, add, next_ref[0])


def add_table_kernel(mesh_rows, mesh_cols, kids, info_ref, notes_ref, out_ref, head, link):
    total = mesh_cols * CAP
    column = info_ref[0]

    def clear(n, carry):
        head[n] = -1
        return carry

    lax.fori_loop(0, 32, clear, 0)

    def source(s, carry):

        def child(k, found):
            count, old, seen = found
            down, across = notes_ref[s, 2 * k], notes_ref[s, 2 * k + 1]
            tile = lax.div(down, mesh_rows) * 4 + lax.div(across, mesh_cols)
            fresh = (lax.rem(across, mesh_cols) == column) & (tile != old) & (tile != seen)

            @pl.when(fresh)
            def _():
                link[count * mesh_cols + s] = head[tile]
                head[tile] = count * mesh_cols + s

            return (
                jnp.where(fresh, count + 1, count),
                jnp.where(fresh, seen, old),
                jnp.where(fresh, tile, seen),
            )

        lax.fori_loop(0, kids, child, (jnp.int32(0), jnp.int32(-1), jnp.int32(-1)))
        return carry

    lax.fori_loop(0, mesh_cols, source, 0)

    def walk(tile, n):
        def one(state):
            n, slot = state
            out_ref[n] = tile
            out_ref[total + n] = slot
            return n + 1, link[slot]

        return lax.while_loop(lambda state: state[1] >= 0, one, (n, head[tile]))[0]

    count = lax.fori_loop(0, 32, walk, jnp.int32(0))
    out_ref[2 * total] = count

    def fill(n, carry):
        last = jnp.maximum(count - 1, 0)
        none = count == 0
        out_ref[n] = jnp.where(none, 0, out_ref[last])
        out_ref[total + n] = jnp.where(none, 0, out_ref[total + last])
        return carry

    lax.fori_loop(count, total, fill, 0)


def add_table(info, notes, mesh_rows, mesh_cols, kids):
    smem = pl.BlockSpec(memory_space=pltpu.SMEM)
    total = mesh_cols * CAP
    return pl.pallas_call(
        functools.partial(add_table_kernel, mesh_rows, mesh_cols, kids),
        out_shape=jax.ShapeDtypeStruct((2 * total + 1,), I32),
        in_specs=[smem, smem],
        out_specs=smem,
        scratch_shapes=[pltpu.SMEM((32,), I32), pltpu.SMEM((total,), I32)],
        name="add_table",
    )(info, notes)


def add_children(table, base, first, second):
    rows, cols = base.shape
    deep = 8

    def row_spec():
        return pl.BlockSpec((BLK, cols), lambda n, t: (n, 0))

    return pl.pallas_call(
        add_kernel,
        out_shape=jax.ShapeDtypeStruct(base.shape, F32),
        grid_spec=pltpu.PrefetchScalarGridSpec(
            num_scalar_prefetch=1,
            grid=(rows // BLK,),
            in_specs=[row_spec()] + [pl.BlockSpec(memory_space=pl.ANY)] * 2,
            out_specs=row_spec(),
            scratch_shapes=[
                pltpu.VMEM((deep, BLK, BLK), F32),
                pltpu.SemaphoreType.DMA((deep,)),
                pltpu.SMEM((1,), I32),
            ],
        ),
        input_output_aliases={1: 0},
        compiler_params=pltpu.CompilerParams(vmem_limit_bytes=32 << 20),
        cost_estimate=pl.CostEstimate(flops=4_000_000, bytes_accessed=24 << 20, transcendentals=0),
        name="add_children",
    )(table, base, first, second)


def on_device(front_matrix, child_blocks, child_target, child_place, child_live):
    mesh_rows = lax.axis_size("row")
    mesh_cols = lax.axis_size("col")
    row = lax.axis_index("row")
    column = lax.axis_index("col")
    x, y, z, core = column // SIDE, column % SIDE, row // 2, row % 2
    slab = front_matrix[:, :BLK]

    offset = jnp.array([0, -1, 1, 2], I32)
    table = jnp.concatenate([(z + offset) % SIDE, row[None], column[None]]).astype(I32)

    strip = exchange(slab[:BLK].reshape(mesh_cols, -1, BLK), "col")[:LEADS]
    late = after(slab, strip)
    rows = slab.shape[0] // SIDE
    piece = spread_x([late[q * rows : (q + 1) * rows] for q in range(SIDE)], x)
    uc = col_pieces(late, core)
    share, four = lead_share(strip, core)
    raw = lax.all_gather(after(piece, four), "col", axis=0, tiled=False)
    packed = map_children(child_blocks, child_target, child_place, child_live, mesh_cols)

    note = jnp.zeros((8, BLK), F32)
    note = note.at[0, : child_target.size].set(child_target.reshape(-1).astype(F32))
    share = after(jnp.concatenate([share, note], axis=0), packed)
    uc = after(uc, four)
    own = to_all(share, "col")
    first, second = packed[:mesh_cols], packed[mesh_cols:]
    first, uc = lax.optimization_barrier((first, uc, own))[:2]
    uc = ring_gather(uc, shift_z)
    first = exchange(first, "col")
    other = swap_cores(own)

    factor, high, low = factor_lead(core[None].astype(I32), own, other)
    notes = after(own, factor)[:, -8, : child_target.size].astype(I32)
    arrivals = add_table(column[None].astype(I32), notes, mesh_rows, mesh_cols, child_target.shape[0])
    second, *uc = lax.optimization_barrier((second, *uc, factor))[:-1]
    second = exchange(second, "col")
    base = update_front(table, uc, raw, front_matrix, factor, high, low)
    return add_children(arrivals, base, first, second)


def solution(mesh):
    return jax.shard_map(
        on_device,
        mesh=mesh,
        in_specs=(
            P("row", "col"),
            P(("row", "col"), None, None),
            P(("row", "col"), None),
            P(("row", "col"), None, None),
            P(("row", "col"), None),
        ),
        out_specs=P("row", "col"),
        check_vma=False,
    )
```

```python
import functools

import jax
import jax.numpy as jnp
from jax import lax
from jax.experimental import pallas as pl
from jax.experimental.pallas import tpu as pltpu
from jax.sharding import PartitionSpec as P

F32 = jnp.float32
BF16 = jnp.bfloat16
I32 = jnp.int32
BLK = 256
LEADS = 4
CAP = 2
SIDE = 4
NB = 128
HIGHEST = lax.Precision.HIGHEST


def dot_nt(left, right, precision=None):
    return lax.dot_general(
        left, right, (((1,), (1,)), ((), ())), precision=precision, preferred_element_type=F32
    )


def dot_nn(left, right, precision=None):
    return lax.dot_general(
        left, right, (((1,), (0,)), ((), ())), precision=precision, preferred_element_type=F32
    )


def split2(value):
    high = value.astype(BF16)
    return high, (value - high.astype(F32)).astype(BF16)


def shift_z(value, dz):
    return lax.ppermute(value, "row", [(r, (r + 2 * dz) % 8) for r in range(8)])


def swap_cores(value):
    return lax.ppermute(value, "row", [(r, r ^ 1) for r in range(8)])


def ring_gather(value, shift):
    return [value, shift(value, 1), shift(value, -1), shift(value, 2)]


def spread_x(parts, x):
    out = jnp.where(x == 0, parts[0], jnp.zeros_like(parts[0]))
    for q in range(1, SIDE):
        out = out + lax.ppermute(parts[q], "col", [(y, q * SIDE + y) for y in range(SIDE)])
    return out


def after(value, *earlier):
    return lax.optimization_barrier((value,) + earlier)[0]


def exchange(value, axis):
    return lax.all_to_all(value, axis, split_axis=0, concat_axis=0, tiled=True)


def to_all(value, axis):
    copies = lax.axis_size(axis)
    return exchange(jnp.broadcast_to(value[None], (copies,) + value.shape), axis)


LOWER = (((0, 0), (1, 0), (2, 0), (3, 0), (1, 1)), ((2, 1), (3, 1), (2, 2), (3, 2), (3, 3)))


def lead_share(strip, core):
    four = to_all(strip, "row")[:LEADS]
    first, second = [jnp.concatenate([four[i, j] for i, j in half], axis=0) for half in LOWER]
    return jnp.where(core == 0, first, second), four


def col_pieces(slab, core):
    blocks = slab.reshape(8, BLK, BLK)
    out = None
    for h in range(2):
        for q in range(2):
            pairs = []
            for r in range(8):
                for j in range(LEADS):
                    pairs.append((r * 16 + j, (2 * j + q) * 16 + r + 8 * h))
            part = jnp.stack([blocks[4 * q + h], blocks[4 * q + 2 + h]])
            part = lax.ppermute(part, ("row", "col"), pairs)
            out = part if out is None else out + part
    other = swap_cores(out)
    return jnp.concatenate(
        [jnp.where(core == 0, out, other), jnp.where(core == 0, other, out)], axis=0
    )


def factor_block(a, u_ref, e_ref):
    n = a.shape[0]
    ri = lax.broadcasted_iota(I32, (n, n), 0)
    ci = lax.broadcasted_iota(I32, (n, n), 1)
    e = jnp.where(ri == ci, F32(1), F32(0))
    base = 0
    for p in range(0, n, 4):
        off = p - base
        m = a.shape[0]
        cols = [jnp.broadcast_to(a[:, p + v : p + v + 1], (m, n)) for v in range(4)]
        s = [[cols[v][off + i : off + i + 1, :] for v in range(4)] for i in range(4)]
        arow = [a[off + i : off + i + 1, :] for i in range(4)]
        erow = [e[off + i : off + i + 1, :] for i in range(4)]
        inverse = []
        for q in range(4):
            r = F32(1) / s[q][q]
            inverse.append(r)
            low = [None] * 4
            for i in range(q + 1, 4):
                low[i] = s[i][q] * r
            for i in range(q + 1, 4):
                for v in range(q + 1, i + 1):
                    s[i][v] = s[i][v] - low[i] * s[v][q]
                arow[i] = arow[i] - low[i] * arow[q]
                erow[i] = erow[i] - low[i] * erow[q]
        for q in range(4):
            scale = lax.rsqrt(s[q][q])
            u_ref[p + q : p + q + 1, :] = arow[q] * scale
            e_ref[p + q : p + q + 1, :] = erow[q] * scale
        following = p + 4
        if following >= n:
            break
        live = None
        if following % 8 == 0:
            cut = following - base
            a, e, cols = a[cut:], e[cut:], [c[cut:] for c in cols]
            base = following
        else:
            live = lax.broadcasted_iota(I32, a.shape, 0) >= following - base
        times = []
        for q in range(4):
            c = cols[q]
            for v in range(q):
                c = c - times[v] * s[q][v]
            times.append(c * inverse[q])
        da = times[0] * arow[0]
        de = times[0] * erow[0]
        for q in range(1, 4):
            da = da + times[q] * arow[q]
            de = de + times[q] * erow[q]
        if live is not None:
            da = jnp.where(live, da, F32(0))
            de = jnp.where(live, de, F32(0))
        a = a - da
        e = e - de


def factor_kernel(table, own_ref, other_ref, l_ref, high_ref, low_ref, m_ref, inv_ref, u_ref, e_ref):
    n = m_ref.shape[0]
    steps = n // NB
    strips = own_ref.shape[0]
    tall = BLK // strips

    def assemble(sources):
        def place(number, carry):
            for half, source in zip(LOWER, sources):
                for spot, (i, j) in enumerate(half):
                    row = pl.multiple_of(i * BLK + number * tall, tall)
                    m_ref[pl.ds(row, tall), j * BLK : (j + 1) * BLK] = source[
                        number, spot * tall : (spot + 1) * tall, :
                    ]
            return carry

        lax.fori_loop(0, strips, place, 0)

    @pl.when(table[0] == 0)
    def _():
        assemble((own_ref, other_ref))

    @pl.when(table[0] != 0)
    def _():
        assemble((other_ref, own_ref))

    l_ref[...] = jnp.zeros_like(l_ref)
    inv_ref[...] = jnp.zeros_like(inv_ref)
    ri = lax.broadcasted_iota(I32, (NB, NB), 0)
    ci = lax.broadcasted_iota(I32, (NB, NB), 1)

    def step(k, carry):
        at = pl.multiple_of(k * NB, NB)
        d = m_ref[pl.ds(at, NB), pl.ds(at, NB)]
        factor_block(jnp.where(ri >= ci, d, d.T), u_ref, e_ref)
        l_ref[pl.ds(at, NB), pl.ds(at, NB)] = jnp.where(ri <= ci, u_ref[...], F32(0)).T
        ik = jnp.where(ri >= ci, e_ref[...], F32(0))
        for kk in range(steps):

            @pl.when(k == kk)
            def _():
                lo, hi = kk * NB, (kk + 1) * NB
                if kk < steps - 1:
                    panel = dot_nt(m_ref[hi:, lo:hi], ik, HIGHEST)
                    l_ref[hi:, lo:hi] = panel
                    m_ref[hi:, hi:] = m_ref[hi:, hi:] - dot_nt(panel, panel, HIGHEST)
                if kk > 0:
                    inv_ref[lo:hi, :lo] = dot_nn(ik, inv_ref[lo:hi, :lo], HIGHEST)
                inv_ref[lo:hi, lo:hi] = ik
                if kk < steps - 1:
                    inv_ref[hi:, :hi] = inv_ref[hi:, :hi] - dot_nn(
                        panel, inv_ref[lo:hi, :hi], HIGHEST
                    )

        return carry

    lax.fori_loop(0, steps, step, 0)
    for i in range(LEADS):
        rows = slice(i * BLK, (i + 1) * BLK)
        high_ref[rows, :], low_ref[rows, :] = split2(inv_ref[rows, :])


def factor_lead(table, *parts):
    n = LEADS * BLK
    vmem = pl.BlockSpec(memory_space=pltpu.VMEM)
    return pl.pallas_call(
        factor_kernel,
        out_shape=(
            jax.ShapeDtypeStruct((n, n), F32),
            jax.ShapeDtypeStruct((n, n), BF16),
            jax.ShapeDtypeStruct((n, n), BF16),
        ),
        in_specs=[pl.BlockSpec(memory_space=pltpu.SMEM)] + [vmem] * 2,
        out_specs=[vmem, vmem, vmem],
        scratch_shapes=[
            pltpu.VMEM((n, n), F32),
            pltpu.VMEM((n, n), F32),
            pltpu.VMEM((NB, NB), F32),
            pltpu.VMEM((NB, NB), F32),
        ],
        compiler_params=pltpu.CompilerParams(vmem_limit_bytes=40 << 20),
        cost_estimate=pl.CostEstimate(flops=60_000_000_000, bytes_accessed=10 << 20, transcendentals=0),
        name="factor_lead",
    )(table, *parts)


def update_kernel(table, *refs):
    uc, raw = refs[0:4], refs[4:8]
    front_ref, own_ref, high_ref, low_ref, out_ref = refs[8:13]
    ch, cl, rh, rl, pan = refs[13:]
    g = pl.program_id(0)
    r, c = table[4], table[5]

    def put(rows, spot, value):
        cols = pl.ds(pl.multiple_of(spot * BLK, BLK), BLK)
        rh[rows, cols], rl[rows, cols] = split2(value)

    upper, lower = slice(0, BLK), slice(BLK, 2 * BLK)

    def solve():
        high, low = rh[...], rl[...]
        out = []
        for j in range(LEADS):
            hi = (j + 1) * BLK
            rows = slice(j * BLK, hi)
            out.append(
                dot_nt(high[:, :hi], high_ref[rows, :hi])
                + (
                    dot_nt(high[:, :hi], low_ref[rows, :hi])
                    + dot_nt(low[:, :hi], high_ref[rows, :hi])
                )
            )
        return out

    @pl.when(g < 2)
    def _():
        for q in range(SIDE):
            put(upper, table[q], uc[q][0])
            put(lower, table[q], uc[q][1])
        got = solve()
        at = pl.ds(pl.multiple_of(g * 2 * BLK, BLK), 2 * BLK)
        for j in range(LEADS):
            cols = slice(j * BLK, (j + 1) * BLK)
            ch[at, cols], cl[at, cols] = split2(got[j])

    @pl.when(g >= 2)
    def _():
        for j in range(LEADS):
            cols = slice(j * BLK, (j + 1) * BLK)
            rh[:, cols], rl[:, cols] = split2(raw[j][0])
        got = solve()
        special = (g == 2) & (r < LEADS)
        top = lax.broadcasted_iota(I32, (2 * BLK, BLK), 0) < BLK
        left = []
        for j in range(LEADS):
            cols = slice(j * BLK, (j + 1) * BLK)
            own = own_ref[:, cols]
            own = jnp.concatenate([own, own], axis=0)
            keep = jnp.where((r >= 2) & (j < 2), F32(1), F32(0))
            left.append(jnp.where(top & special, own * keep, got[j]))

            @pl.when(c == j)
            def _():
                pan[...] = jnp.where(top & special, own, got[j])

        left_h, left_l = split2(jnp.concatenate(left, axis=1))
        for t in range(4):
            rows = slice(t * BLK, (t + 1) * BLK)
            right_h, right_l = ch[rows, :], cl[rows, :]
            out_ref[:, rows] = front_ref[:, rows] - (
                dot_nt(left_h, right_h) + (dot_nt(left_h, right_l) + dot_nt(left_l, right_h))
            )

        @pl.when(c < LEADS)
        def _():
            out_ref[:, :BLK] = pan[...]


def update_front(table, uc, raw, front, factor, high, low):
    n = LEADS * BLK
    rows, cols = front.shape
    tall = 2 * BLK

    def step(g):
        return jnp.maximum(g - 2, 0)

    def tall_spec():
        return pl.BlockSpec((tall, cols), lambda g, t: (step(g), 0))

    def raw_spec(j):
        return pl.BlockSpec((1, tall, BLK), lambda g, t: (step(g) * SIDE + j, 0, 0))

    in_specs = [pl.BlockSpec((2, BLK, BLK), lambda g, t: (jnp.minimum(g, 1), 0, 0))] * SIDE
    in_specs += [raw_spec(j) for j in range(LEADS)]
    in_specs += [
        tall_spec(),
        pl.BlockSpec((BLK, n), lambda g, t: (jnp.minimum(t[4], LEADS - 1), 0)),
        pl.BlockSpec((n, n), lambda g, t: (0, 0)),
        pl.BlockSpec((n, n), lambda g, t: (0, 0)),
    ]
    return pl.pallas_call(
        update_kernel,
        out_shape=jax.ShapeDtypeStruct((rows, cols), F32),
        grid_spec=pltpu.PrefetchScalarGridSpec(
            num_scalar_prefetch=1,
            grid=(2 + rows // tall,),
            in_specs=in_specs,
            out_specs=tall_spec(),
            scratch_shapes=[
                pltpu.VMEM((n, n), BF16),
                pltpu.VMEM((n, n), BF16),
                pltpu.VMEM((tall, n), BF16),
                pltpu.VMEM((tall, n), BF16),
                pltpu.VMEM((tall, BLK), F32),
            ],
        ),
        compiler_params=pltpu.CompilerParams(vmem_limit_bytes=58 << 20),
        cost_estimate=pl.CostEstimate(flops=26_000_000_000, bytes_accessed=36 << 20, transcendentals=0),
        name="update_front",
    )(table, *uc, *([raw] * LEADS), front, factor, high, low)


def slots_of(target, mesh_cols):
    kids = target.shape[-2]
    same = jnp.all(target[..., :, None, :] == target[..., None, :, :], axis=-1)
    number = jnp.arange(kids, dtype=I32)
    first = jnp.min(jnp.where(same, number, kids), axis=-1)
    leads = first == number
    goal = target[..., 1] % mesh_cols
    alike = (goal[..., :, None] == goal[..., None, :]) & leads[..., None, :]
    rank = jnp.sum((alike & (number < first[..., :, None])).astype(I32), axis=-1)
    return rank * mesh_cols + goal, leads


def sort_order(keys):
    count = keys.shape[0]
    number = jnp.arange(count, dtype=I32)
    before = (keys[None, :] < keys[:, None]) | (
        (keys[None, :] == keys[:, None]) & (number[None, :] < number[:, None])
    )
    place = jnp.sum(before.astype(I32), axis=1)
    hot = (place[None, :] == number[:, None]).astype(I32)
    return lambda values: jnp.sum(hot * values[None, :], axis=1)


def map_kernel(table, block_ref, place_ref, first_ref, second_ref):
    k = pl.program_id(0)
    live_row, live_col = table[16 + k], table[24 + k]
    target = lax.broadcasted_iota(I32, (BLK, BLK), 0)
    source = lax.broadcasted_iota(I32, (BLK, BLK), 1)

    def picks(index, live):
        hit = (place_ref[0, index : index + 1, :] == target) & (source < live)
        return jnp.where(hit, F32(1), F32(0)).astype(BF16)

    def parts(value):
        high = value.astype(BF16)
        rest = value - high.astype(F32)
        middle = rest.astype(BF16)
        return high, middle, (rest - middle.astype(F32)).astype(BF16)

    row_pick, col_pick = picks(0, live_row), picks(1, live_col)
    high, middle, low = parts(block_ref[0])
    moved = dot_nn(row_pick, high) + (dot_nn(row_pick, middle) + dot_nn(row_pick, low))
    high, middle, low = parts(moved)
    mapped = dot_nt(high, col_pick) + (dot_nt(middle, col_pick) + dot_nt(low, col_pick))
    opens = (k == 0) | (table[8 + k] != table[8 + jnp.maximum(k - 1, 0)])

    early = table[8 + k] < table[48]
    for out_ref, mine in ((first_ref, early), (second_ref, jnp.logical_not(early))):

        @pl.when(mine & opens)
        def _():
            out_ref[0] = mapped

        @pl.when(mine & jnp.logical_not(opens))
        def _():
            out_ref[0] = out_ref[0] + mapped


def map_children(child_blocks, child_target, child_place, child_live, mesh_cols):
    kids = child_blocks.shape[0]
    slot, _ = slots_of(child_target, mesh_cols)
    ordered = sort_order(slot)
    spots = ordered(slot)
    early = spots < mesh_cols
    last = jnp.max(jnp.where(early, spots, 0))
    opening = jnp.min(jnp.where(early, mesh_cols, spots - mesh_cols)) % mesh_cols
    table = jnp.concatenate(
        [
            ordered(jnp.arange(kids, dtype=I32)),
            spots,
            ordered(child_live[:, 0]),
            ordered(child_live[:, 1]),
            jnp.where(early, spots, last),
            jnp.where(early, opening, spots - mesh_cols),
            jnp.full((1,), mesh_cols, I32),
        ]
    )
    return pl.pallas_call(
        map_kernel,
        out_shape=[jax.ShapeDtypeStruct((mesh_cols, BLK, BLK), F32)] * CAP,
        grid_spec=pltpu.PrefetchScalarGridSpec(
            num_scalar_prefetch=1,
            grid=(kids,),
            in_specs=[
                pl.BlockSpec((1, BLK, BLK), lambda k, t: (t[k], 0, 0)),
                pl.BlockSpec((1, 2, BLK), lambda k, t: (t[k], 0, 0)),
            ],
            out_specs=[
                pl.BlockSpec((1, BLK, BLK), lambda k, t: (t[32 + k], 0, 0)),
                pl.BlockSpec((1, BLK, BLK), lambda k, t: (t[40 + k], 0, 0)),
            ],
        ),
        cost_estimate=pl.CostEstimate(flops=2_000_000_000, bytes_accessed=4 << 20, transcendentals=0),
        name="map_children",
    )(table, child_blocks, child_place)


def add_kernel(table, base_ref, first_ref, second_ref, out_ref, buffers, sems, next_ref):
    row = pl.program_id(0)
    total = 32
    count = table[2 * total]
    deep = buffers.shape[0]
    parts = (first_ref, second_ref)
    each = total // len(parts)

    def copy(n, part, at):
        k = lax.rem(n, deep)
        return pltpu.make_async_copy(part.at[at], buffers.at[k], sems.at[k])

    def start(n):
        slot = table[total + n]
        for q, part in enumerate(parts):

            @pl.when(lax.div(slot, each) == q)
            def _():
                copy(n, part, slot - q * each).start()

    @pl.when(row == 0)
    def _():
        next_ref[0] = 0
        for n in range(deep):

            @pl.when(n < count)
            def _():
                start(jnp.int32(n))

    out_ref[...] = base_ref[...]

    def here(n):
        return (n < count) & (lax.div(table[jnp.minimum(n, total - 1)], 4) == row)

    def add(n):
        copy(n, first_ref, 0).wait()
        cols = pl.ds(pl.multiple_of(lax.rem(table[n], 4) * BLK, BLK), BLK)
        out_ref[:, cols] = out_ref[:, cols] + buffers[lax.rem(n, deep)]

        @pl.when(n + deep < count)
        def _():
            start(n + deep)

        return n + 1

    next_ref[0] = lax.while_loop(here, add, next_ref[0])


def add_table_kernel(mesh_rows, mesh_cols, kids, info_ref, notes_ref, out_ref, head, link):
    total = mesh_cols * CAP
    column = info_ref[0]

    def clear(n, carry):
        head[n] = -1
        return carry

    lax.fori_loop(0, 32, clear, 0)

    def source(s, carry):

        def child(k, found):
            count, old, seen = found
            down, across = notes_ref[s, 2 * k], notes_ref[s, 2 * k + 1]
            tile = lax.div(down, mesh_rows) * 4 + lax.div(across, mesh_cols)
            fresh = (lax.rem(across, mesh_cols) == column) & (tile != old) & (tile != seen)

            @pl.when(fresh)
            def _():
                link[count * mesh_cols + s] = head[tile]
                head[tile] = count * mesh_cols + s

            return (
                jnp.where(fresh, count + 1, count),
                jnp.where(fresh, seen, old),
                jnp.where(fresh, tile, seen),
            )

        lax.fori_loop(0, kids, child, (jnp.int32(0), jnp.int32(-1), jnp.int32(-1)))
        return carry

    lax.fori_loop(0, mesh_cols, source, 0)

    def walk(tile, n):
        def one(state):
            n, slot = state
            out_ref[n] = tile
            out_ref[total + n] = slot
            return n + 1, link[slot]

        return lax.while_loop(lambda state: state[1] >= 0, one, (n, head[tile]))[0]

    count = lax.fori_loop(0, 32, walk, jnp.int32(0))
    out_ref[2 * total] = count

    def fill(n, carry):
        last = jnp.maximum(count - 1, 0)
        none = count == 0
        out_ref[n] = jnp.where(none, 0, out_ref[last])
        out_ref[total + n] = jnp.where(none, 0, out_ref[total + last])
        return carry

    lax.fori_loop(count, total, fill, 0)


def add_table(info, notes, mesh_rows, mesh_cols, kids):
    smem = pl.BlockSpec(memory_space=pltpu.SMEM)
    total = mesh_cols * CAP
    return pl.pallas_call(
        functools.partial(add_table_kernel, mesh_rows, mesh_cols, kids),
        out_shape=jax.ShapeDtypeStruct((2 * total + 1,), I32),
        in_specs=[smem, smem],
        out_specs=smem,
        scratch_shapes=[pltpu.SMEM((32,), I32), pltpu.SMEM((total,), I32)],
        name="add_table",
    )(info, notes)


def add_children(table, base, first, second):
    rows, cols = base.shape
    deep = 8

    def row_spec():
        return pl.BlockSpec((BLK, cols), lambda n, t: (n, 0))

    return pl.pallas_call(
        add_kernel,
        out_shape=jax.ShapeDtypeStruct(base.shape, F32),
        grid_spec=pltpu.PrefetchScalarGridSpec(
            num_scalar_prefetch=1,
            grid=(rows // BLK,),
            in_specs=[row_spec()] + [pl.BlockSpec(memory_space=pl.ANY)] * 2,
            out_specs=row_spec(),
            scratch_shapes=[
                pltpu.VMEM((deep, BLK, BLK), F32),
                pltpu.SemaphoreType.DMA((deep,)),
                pltpu.SMEM((1,), I32),
            ],
        ),
        input_output_aliases={1: 0},
        compiler_params=pltpu.CompilerParams(vmem_limit_bytes=32 << 20),
        cost_estimate=pl.CostEstimate(flops=4_000_000, bytes_accessed=24 << 20, transcendentals=0),
        name="add_children",
    )(table, base, first, second)


def on_device(front_matrix, child_blocks, child_target, child_place, child_live):
    mesh_rows = lax.axis_size("row")
    mesh_cols = lax.axis_size("col")
    row = lax.axis_index("row")
    column = lax.axis_index("col")
    x, y, z, core = column // SIDE, column % SIDE, row // 2, row % 2
    slab = front_matrix[:, :BLK]

    offset = jnp.array([0, -1, 1, 2], I32)
    table = jnp.concatenate([(z + offset) % SIDE, row[None], column[None]]).astype(I32)

    strip = exchange(slab[:BLK].reshape(mesh_cols, -1, BLK), "col")[:LEADS]
    late = after(slab, strip)
    rows = slab.shape[0] // SIDE
    piece = spread_x([late[q * rows : (q + 1) * rows] for q in range(SIDE)], x)
    uc = col_pieces(late, core)
    share, four = lead_share(strip, core)
    raw = lax.all_gather(after(piece, four), "col", axis=0, tiled=False)
    first, second = map_children(child_blocks, child_target, child_place, child_live, mesh_cols)

    note = jnp.zeros((8, BLK), F32)
    note = note.at[0, : child_target.size].set(child_target.reshape(-1).astype(F32))
    share, first, second = lax.optimization_barrier(
        (jnp.concatenate([share, note], axis=0), first, second)
    )
    uc = after(uc, four)
    own = to_all(share, "col")
    first, uc = lax.optimization_barrier((first, uc, own))[:2]
    uc = ring_gather(uc, shift_z)
    first = exchange(first, "col")
    other = swap_cores(own)

    factor, high, low = factor_lead(core[None].astype(I32), own, other)
    notes = after(own, factor)[:, -8, : child_target.size].astype(I32)
    arrivals = add_table(column[None].astype(I32), notes, mesh_rows, mesh_cols, child_target.shape[0])
    second, *uc = lax.optimization_barrier((second, *uc, factor))[:-1]
    second = exchange(second, "col")
    base = update_front(table, uc, raw, front_matrix, factor, high, low)
    return add_children(arrivals, base, first, second)


def solution(mesh):
    return jax.shard_map(
        on_device,
        mesh=mesh,
        in_specs=(
            P("row", "col"),
            P(("row", "col"), None, None),
            P(("row", "col"), None),
            P(("row", "col"), None, None),
            P(("row", "col"), None),
        ),
        out_specs=P("row", "col"),
        check_vma=False,
    )
```
